128 devices in a mesh: dom: 128 (over z, y, x, core).
Axes of the slice: x: 4, y: 4, z: 4, core: 2. Of those that a mesh axis runs over, the one named last changes fastest.
Arguments:
- positions: float32 [3, 65536, 128], P(None, 'dom'), may hold values from 0 to 1
- velocities: float32 [3, 65536, 128], P(None, 'dom'), may hold values from -3 to 3
- masses: float32 [65536, 128], P('dom'), may hold values from 4.8828126e-05 to 0.00048828125
- active_leaves: int32 [2048], P('dom'), may hold values from 0 to 511, as said below
- active_count: int32 [128], P('dom'), may hold values from 4 to 16, as said below
- partner_owner: int32 [2048, 16], P('dom'), may hold values from 0 to 127, as said below
- partner_leaf: int32 [2048, 16], P('dom'), may hold values from 0 to 511, as said below
- mig_leaf: int32 [2048], P('dom'), may hold values from -1 to 511
Outputs:
- new_positions: float32 [3, 65536, 128], P(None, 'dom')
- new_velocities: float32 [3, 65536, 128], P(None, 'dom')
- arrived: float32 [7, 2048, 128], P(None, 'dom')
The draws below stay inside these ranges and needn't reach their ends.
Inputs may be any that keep to these rules, and one draw needn't show every extreme that they name: `active_leaves`: within one domain's 16 slots the leaf numbers are distinct. `active_count`: at most 16; some domain has exactly 16. `partner_owner`: the owner lies within 2 domains of the list's own domain, counted cyclically along the curve. `partner_leaf`: for each domain and each other domain within reach, its lists name exactly 8 distinct leaves of that domain. `mig_leaf`: -1 marks an empty slot.
All inputs are finite; a program needn't handle non-finite values.
Results may differ from the reference program's by a relative error of at most 0.00002.
Values sent between devices are 32-bit elements; how exact they have to be, the bound alone decides.
No kernel may reach another device: no remote copies, remote signals or barrier semaphores. Data moves between devices by JAX's collectives and lax.ppermute only.
A program may use at most 64 MiB of HBM per device.

```python
import math
import jax
import jax.numpy as jnp
from jax import lax

LEAF = 128
LEAVES = 512
ACT = 16
PARTNERS = 16
REACH = 2
IMPORT = 8
SLOTS = 4
NLEAF = 65536
ACTIVE = 2048
MIGR = 2048


def domain_lists(key, domain):
    inner = jax.random.fold_in(jax.random.fold_in(key, 71), domain)
    entries = ACT * PARTNERS
    fixed_count = 2 * REACH * IMPORT
    candidates = jax.vmap(lambda n: jax.random.permutation(jax.random.fold_in(inner, 100 + n), LEAVES)[:IMPORT])(jnp.arange(2 * REACH))
    index = jnp.arange(entries)
    free_side = jax.random.randint(jax.random.fold_in(inner, 1), (entries,), 0, 2 * REACH + 1)
    side = jnp.where(index < fixed_count, index // IMPORT, free_side)
    pick = jnp.where(index < fixed_count, index % IMPORT, jax.random.randint(jax.random.fold_in(inner, 2), (entries,), 0, IMPORT))
    local_leaf = jax.random.randint(jax.random.fold_in(inner, 3), (entries,), 0, LEAVES)
    is_local = side == 2 * REACH
    safe_side = jnp.minimum(side, 2 * REACH - 1)
    remote_leaf = candidates[safe_side, pick]
    offset = jnp.where(safe_side < REACH, safe_side - REACH, safe_side - REACH + 1)
    offset = jnp.where(is_local, 0, offset)
    leaf = jnp.where(is_local, local_leaf, remote_leaf)
    order = jax.random.permutation(jax.random.fold_in(inner, 4), entries)
    domains = ACTIVE // ACT
    owner = jnp.mod(domain + offset, domains)
    return (owner[order].reshape(ACT, PARTNERS).astype(jnp.int32), leaf[order].reshape(ACT, PARTNERS).astype(jnp.int32))


def all_lists(key):
    domains = ACTIVE // ACT
    owner, leaf = jax.vmap(lambda d: domain_lists(key, d))(jnp.arange(domains))
    return (owner.reshape(ACTIVE, PARTNERS), leaf.reshape(ACTIVE, PARTNERS))


def draw_partner_owner(key, part):
    return all_lists(key)[0]


def draw_partner_leaf(key, part):
    return all_lists(key)[1]


def draw_active_leaves(key, part):
    domains = ACTIVE // ACT
    inner = jax.random.fold_in(key, 5)
    rows = jax.vmap(lambda d: jax.random.permutation(jax.random.fold_in(inner, d), LEAVES)[:ACT])(jnp.arange(domains))
    return rows.reshape(ACTIVE).astype(jnp.int32)


def draw_active_count(key, part):
    domains = ACTIVE // ACT
    base = jax.random.randint(jax.random.fold_in(key, 9), (domains,), ACT // 4, ACT // 2 + 1)
    fullest = jax.random.randint(jax.random.fold_in(key, 11), (), 0, domains)
    return jnp.where(jnp.arange(domains) == fullest, ACT, base).astype(jnp.int32)


def plant(array, stream_key, least, largest):
    longest = array.shape.index(max(array.shape))
    spots = []
    for shift in (0, 1):
        where = [jax.random.randint(jax.random.fold_in(stream_key, axis), (), 0, length) for axis, length in enumerate(array.shape)]
        where[longest] = (where[longest] + shift) % array.shape[longest]
        spots.append(tuple(where))
    return array.at[spots[0]].set(least).at[spots[1]].set(largest)


def shard_levels(rng, extent, pieces, least, high):
    def one(position, blocks):
        heights = jax.random.uniform(jax.random.fold_in(jax.random.fold_in(rng, 6), position), (blocks,), jnp.float32, least / len(pieces), high / len(pieces))
        return jnp.repeat(jnp.exp(heights), extent[position] // blocks).reshape((-1,) + (1,) * (len(extent) - position - 1))

    level = one(*pieces[0])
    for cut in pieces[1:]:
        level = level * one(*cut)
    return level


def normal_values(key, extent, spread, reach, pieces=(), held_as=jnp.bfloat16):
    values = jax.random.normal(key, extent, jnp.float32) * spread
    if len(pieces) > 0:
        values = shard_levels(key, extent, pieces, -0.22, 0.18) * values
    return jnp.clip(values, min=-reach, max=reach).astype(held_as)


def setup_inputs(seed: int = 0) -> dict:
    key_list = jax.random.split(jax.random.key(seed), 9)
    return {
        "positions": jnp.clip(1.0 * jax.random.uniform(key_list[0], (3, NLEAF, LEAF), jnp.float32) ** shard_levels(key_list[0], (3, NLEAF, LEAF), ((1, 128),), -0.2, 0.2), 0.0, 1.0),
        "velocities": normal_values(key_list[1], (3, NLEAF, LEAF), 0.5, 3.0, ((1, 128),), jnp.float32),
        "masses": jnp.clip(jnp.exp(math.log(0.00048828125) - 2.3025851 * jax.random.uniform(key_list[2], (NLEAF, LEAF), jnp.float32) ** shard_levels(key_list[2], (NLEAF, LEAF), ((0, 128),), -0.2, 0.2)), 4.882812572759576e-05, 0.00048828125),
        "active_leaves": draw_active_leaves(jax.random.fold_in(key_list[8], 71), 0),
        "active_count": draw_active_count(jax.random.fold_in(key_list[8], 71), 0),
        "partner_owner": draw_partner_owner(jax.random.fold_in(key_list[8], 71), 0),
        "partner_leaf": draw_partner_leaf(jax.random.fold_in(key_list[8], 71), 0),
        "mig_leaf": plant(jax.random.randint(key_list[7], (MIGR,), -1, LEAVES), jax.random.fold_in(key_list[7], 1), -1, LEAVES - 1).astype(jnp.int32),
    }


time_step = 0.25
soften = 0.02
split_scale = 0.25

def pair_accel(target, source, weight):
    delta = source[:, :, None, :] - target[:, None, :, None]
    square = delta[0] * delta[0] + delta[1] * delta[1] + delta[2] * delta[2] + soften * soften
    inverse = lax.rsqrt(square)
    scaled = square * inverse / (2.0 * split_scale)
    factor = jax.scipy.special.erfc(scaled) + 2.0 / math.sqrt(math.pi) * scaled * jnp.exp(-scaled * scaled)
    strength = weight[:, None, :] * factor * inverse * inverse * inverse
    return lax.optimization_barrier(jnp.sum(strength[None] * delta, axis=(1, 3)))

def reference(positions, velocities, masses, active_leaves, active_count, partner_owner, partner_leaf, mig_leaf):
    domains = NLEAF // LEAVES
    slot_ids = jnp.arange(ACTIVE, dtype=jnp.int32)
    targets = slot_ids // ACT * LEAVES + active_leaves
    sources = partner_owner * LEAVES + partner_leaf

    def one_slot(pair):
        target_id, source_ids = pair
        return pair_accel(positions[:, target_id, :], positions[:, source_ids, :], masses[source_ids])
    accel = lax.map(one_slot, (targets, sources))
    live = slot_ids % ACT < active_count[slot_ids // ACT]
    accel = jnp.where(live[:, None, None], accel, jnp.float32(0.0))
    new_velocities = velocities.at[:, targets, :].add(jnp.moveaxis(time_step * accel, 1, 0))
    new_positions = positions + time_step * new_velocities
    state = jnp.concatenate([new_positions, new_velocities, masses[None]], axis=0)
    table = mig_leaf.reshape(domains, 2 * REACH, SLOTS)
    owners = jnp.arange(domains, dtype=jnp.int32)[:, None, None] * LEAVES
    blocks = state[:, owners + jnp.maximum(table, 0), :]
    blocks = blocks * jnp.where(table >= 0, 1.0, 0.0).astype(jnp.float32)[None, :, :, :, None]
    offsets = [o for o in range(-REACH, REACH + 1) if o != 0]
    moved = [jnp.roll(blocks[:, :, n], offsets[n], axis=1) for n in range(2 * REACH)]
    arrived = jnp.stack(moved, axis=2).reshape(7, MIGR, LEAF)
    return (new_positions, new_velocities, arrived)
```

```python
import functools
import math

import jax
import jax.numpy as jnp
from jax import lax
from jax.experimental import pallas as pl
from jax.experimental.pallas import tpu as pltpu
from jax.sharding import PartitionSpec as P

REACH = 2
SLOTS = 4
IMPORT = 8
ACT = 16
PARTNERS = 16
LANES = 128
SIDES = 2 * REACH
IMPORTS = SIDES * IMPORT
BIG = 1 << 20
OFFSETS = [o for o in range(-REACH, REACH + 1) if o != 0]

soften = 0.02
EPS = 4.0 * soften * soften
NEG_LOG2E = -math.log2(math.e)
TWO_OVER_ROOT_PI = 2.0 / math.sqrt(math.pi)

REMOTE, LOCAL, N_REMOTE, N_LOCAL, ORDER, COUNTS, FROM = 0, 256, 512, 528, 544, 560, 576
PLAN = 592

VMEM = pl.BlockSpec(memory_space=pltpu.VMEM)
SMEM = pl.BlockSpec(memory_space=pltpu.SMEM)
F32, I32 = jnp.float32, jnp.int32


def params(mib):
    return pltpu.CompilerParams(vmem_limit_bytes=mib << 20)


def shifted(shard, by):
    length = lax.axis_size("dom")
    return lax.ppermute(shard, "dom", [(i, (i + by) % length) for i in range(length)])


def request_kernel(domains, me_ref, owner_ref, leaf_ref, *outs):
    requests, map_ref, mult_ref = outs[:SIDES], outs[SIDES], outs[SIDES + 1]
    leaf = leaf_ref[...]
    relative = owner_ref[...] - me_ref[0] + REACH
    relative = jnp.where(relative < 0, relative + domains, relative)
    relative = jnp.where(relative >= domains, relative - domains, relative)
    lane = lax.broadcasted_iota(I32, (1, LANES), 1)
    place = IMPORTS + leaf
    for side, offset in enumerate(OFFSETS):
        mine = relative == offset + REACH
        key = jnp.where(mine, leaf, BIG)
        rank = jnp.zeros_like(leaf)
        row = jnp.zeros((1, LANES), I32)
        for k in range(IMPORT):
            least = jnp.min(jnp.min(key, axis=0, keepdims=True), axis=1, keepdims=True)
            row = jnp.where(lane == k, jnp.broadcast_to(least, row.shape), row)
            here = key == least
            rank = jnp.where(here, k, rank)
            key = jnp.where(here, BIG, key)
        requests[side][...] = jnp.minimum(row, 511)
        place = jnp.where(mine, side * IMPORT + rank, place)
    map_ref[...] = place
    column = lax.broadcasted_iota(I32, place.shape, 1)
    times = jnp.zeros_like(place)
    earlier = jnp.zeros_like(place)
    for k in range(PARTNERS):
        same = (place == place[:, k : k + 1]).astype(I32)
        times = times + same
        earlier = jnp.where(column > k, earlier + same, earlier)
    mult_ref[...] = jnp.where(earlier > 0, 0, times)


def plan_kernel(map_ref, mult_ref, active_ref, count_ref, mig_ref, plan_ref):
    live = count_ref[0]

    def one_slot(a, tally):
        first, last = tally

        def entry(k, sizes):
            n_remote, n_local = sizes
            place = map_ref[a, k]
            times = mult_ref[a, k]
            is_remote = place < IMPORTS
            word = place * 32 + times
            plan_ref[REMOTE + a * PARTNERS + n_remote] = word
            plan_ref[LOCAL + a * PARTNERS + n_local] = word - IMPORTS * 32
            counts = times > 0
            return (
                n_remote + jnp.where(counts & is_remote, 1, 0),
                n_local + jnp.where(counts & ~is_remote, 1, 0),
            )

        sizes = (jnp.int32(0), jnp.int32(0))
        for k in range(PARTNERS - 1):
            sizes = entry(k, sizes)
        k = PARTNERS - 1
        n_remote, n_local = sizes
        place, times = map_ref[a, k], mult_ref[a, k]
        remote_last = (times > 0) & (place < IMPORTS)
        local_last = (times > 0) & (place >= IMPORTS)

        @pl.when(remote_last)
        def _():
            plan_ref[REMOTE + a * PARTNERS + n_remote] = place * 32 + times

        @pl.when(local_last)
        def _():
            plan_ref[LOCAL + a * PARTNERS + n_local] = (place - IMPORTS) * 32 + times

        plan_ref[N_REMOTE + a] = n_remote + jnp.where(remote_last, 1, 0)
        plan_ref[N_LOCAL + a] = n_local + jnp.where(local_last, 1, 0)
        leaf = active_ref[a]
        leaves_home = jnp.int32(0)
        for n in range(SIDES * SLOTS):
            hit = mig_ref[n] == leaf
            leaves_home = leaves_home | jnp.where(hit, 1, 0)

            @pl.when(hit)
            def _():
                plan_ref[FROM + n] = a

        plan_ref[ORDER + jnp.where(leaves_home > 0, first, last)] = a
        return (first + leaves_home, last - (1 - leaves_home))

    for n in range(SIDES * SLOTS):
        plan_ref[FROM + n] = -1
    first, _ = lax.fori_loop(0, live, one_slot, (jnp.int32(0), live - 1))
    plan_ref[COUNTS] = first
    plan_ref[COUNTS + 1] = live


def reply_kernel(r0, r1, r2, r3, positions_ref, masses_ref, o0, o1, o2, o3):
    for request, out in ((r0, o0), (r1, o1), (r2, o2), (r3, o3)):
        for k in range(IMPORT):
            leaf = request[0, k]
            for c in range(3):
                out[4 * k + c : 4 * k + c + 1, :] = 2.0 * positions_ref[c, pl.ds(leaf, 1), :]
            out[4 * k + 3 : 4 * k + 4, :] = masses_ref[pl.ds(leaf, 1), :]


def set_targets(targets, positions_ref, leaf):
    for c in range(3):
        row = 2.0 * positions_ref[c, pl.ds(leaf, 1), :]
        targets[c] = jnp.transpose(jnp.broadcast_to(row, (LANES, LANES)))


def add_pairs(targets, total, sources):
    wide = [[jnp.broadcast_to(v, (8, LANES)) for v in source] for source in sources]
    for g in range(LANES // 8):
        rows = slice(8 * g, 8 * g + 8)
        tx, ty, tz = (targets[c, rows, :] for c in range(3))
        ax = ay = az = None
        for x, y, z, m, mc in wide:
            dx, dy, dz = x - tx, y - ty, z - tz
            square = dx * dx + dy * dy + (dz * dz + EPS)
            inverse = lax.rsqrt(square)
            gauss = mc * jnp.exp2(square * NEG_LOG2E)
            tail = (1.0 - lax.erf(square * inverse)) * (m * inverse)
            strength = (tail + gauss) * (inverse * inverse)
            px, py, pz = strength * dx, strength * dy, strength * dz
            ax, ay, az = (px, py, pz) if ax is None else (ax + px, ay + py, az + pz)
        total[0, rows, :] += ax
        total[1, rows, :] += ay
        total[2, rows, :] += az


def add_list(targets, total, plan_ref, base, n, row_of):
    def some(start, many):
        sources = []
        for q in range(many):
            word = plan_ref[base + start + q]
            x, y, z, m = row_of(lax.shift_right_logical(word, 5))
            m = m * (word & 31).astype(F32)
            sources.append((x, y, z, m, m * TWO_OVER_ROOT_PI))
        add_pairs(targets, total, sources)

    fours = lax.shift_right_logical(n, 2)

    @pl.loop(0, fours)
    def _(q):
        some(4 * q, 4)

    @pl.when((n & 2) > 0)
    def _():
        some(4 * fours, 2)

    @pl.when((n & 1) > 0)
    def _():
        some(n - 1, 1)


def lane_sums(total):
    ones = jnp.ones((8, LANES), F32)
    return [
        lax.dot_general(
            ones,
            total[c],
            (((1,), (1,)), ((), ())),
            precision=lax.Precision.HIGHEST,
            preferred_element_type=F32,
        )[0:1]
        for c in range(3)
    ]


def local_kernel(plan_ref, active_ref, positions_ref, masses_ref, _, kick_ref, targets, total):
    kick_ref[...] = jnp.zeros_like(kick_ref)

    def row_of(leaf):
        at = pl.ds(leaf, 1)
        return [2.0 * positions_ref[c, at, :] for c in range(3)] + [masses_ref[at, :]]

    @pl.loop(0, plan_ref[COUNTS + 1])
    def _(a):
        n = plan_ref[N_LOCAL + a]

        @pl.when(n > 0)
        def _():
            set_targets(targets, positions_ref, active_ref[a])
            total[...] = jnp.zeros_like(total)
            add_list(targets, total, plan_ref, LOCAL + a * PARTNERS, n, row_of)
            for c, row in enumerate(lane_sums(total)):
                kick_ref[a, c : c + 1, :] = row


def remote_slots(lo, hi, plan_ref, active_ref, positions_ref, imports, kick_ref, targets, total):
    def row_of(place):
        return [imports[pl.ds(4 * place + c, 1), :] for c in range(4)]

    @pl.loop(lo, hi)
    def _(q):
        a = plan_ref[ORDER + q]
        set_targets(targets, positions_ref, active_ref[a])
        total[...] = jnp.zeros_like(total)
        add_list(targets, total, plan_ref, REMOTE + a * PARTNERS, plan_ref[N_REMOTE + a], row_of)
        for c, row in enumerate(lane_sums(total)):
            kick_ref[a, c : c + 1, :] += row


def gather_imports(received, imports):
    for side, ref in enumerate(received):
        imports[side * 4 * IMPORT : (side + 1) * 4 * IMPORT, :] = ref[...]


def leaving_kernel(plan_ref, active_ref, mig_ref, positions_ref, velocities_ref, masses_ref, kick_in, r0, r1, r2, r3,
                   kick_ref, b0, b1, b2, b3, imports, targets, total):
    gather_imports((r0, r1, r2, r3), imports)
    kick_ref[...] = kick_in[...]
    remote_slots(0, plan_ref[COUNTS], plan_ref, active_ref, positions_ref, imports, kick_ref, targets, total)
    for side, block in enumerate((b0, b1, b2, b3)):
        for k in range(SLOTS):
            n = side * SLOTS + k
            leaf = mig_ref[n]
            at = pl.ds(jnp.maximum(leaf, 0), 1)
            held = jnp.full((1, LANES), jnp.where(leaf >= 0, 1, 0), I32) > 0
            a = plan_ref[FROM + n]
            kicked = jnp.full((1, LANES), jnp.where(a >= 0, 1, 0), I32) > 0
            for c in range(3):
                kick = jnp.where(kicked, kick_ref[jnp.maximum(a, 0), c : c + 1, :], 0.0)
                v = velocities_ref[c, at, :] + kick
                x = positions_ref[c, at, :] + 0.25 * v
                block[c, k : k + 1, :] = jnp.where(held, x, 0.0)
                block[3 + c, k : k + 1, :] = jnp.where(held, v, 0.0)
            block[6, k : k + 1, :] = jnp.where(held, masses_ref[at, :], 0.0)


def staying_kernel(plan_ref, active_ref, positions_ref, velocities_ref, kick_in, r0, r1, r2, r3,
                   new_positions, new_velocities, kick_ref, imports, targets, total):
    gather_imports((r0, r1, r2, r3), imports)
    kick_ref[...] = kick_in[...]
    new_velocities[...] = velocities_ref[...]
    new_positions[...] = positions_ref[...] + 0.25 * velocities_ref[...]
    live = plan_ref[COUNTS + 1]
    remote_slots(plan_ref[COUNTS], live, plan_ref, active_ref, positions_ref, imports, kick_ref, targets, total)

    @pl.loop(0, live)
    def _(a):
        at = pl.ds(active_ref[a], 1)
        for c in range(3):
            v = velocities_ref[c, at, :] + kick_ref[a, c : c + 1, :]
            new_velocities[c, at, :] = v
            new_positions[c, at, :] = positions_ref[c, at, :] + 0.25 * v


def shape(*dims, dtype=F32):
    return jax.ShapeDtypeStruct(dims, dtype)


def per_device(positions, velocities, masses, active_leaves, active_count, partner_owner, partner_leaf, mig_leaf):
    leaves = positions.shape[1]
    domains = lax.axis_size("dom")
    me = lax.axis_index("dom").astype(I32).reshape(1)
    *requests, place, times = pl.pallas_call(
        functools.partial(request_kernel, domains),
        out_shape=[shape(1, LANES, dtype=I32)] * SIDES + [shape(ACT, PARTNERS, dtype=I32)] * 2,
        in_specs=[SMEM, VMEM, VMEM],
        out_specs=[VMEM] * (SIDES + 2),
        compiler_params=params(4),
        name="requests",
    )(me, partner_owner, partner_leaf)
    asked = [shifted(r, o) for r, o in zip(requests, OFFSETS)]
    plan = pl.pallas_call(
        plan_kernel,
        out_shape=shape(PLAN, dtype=I32),
        in_specs=[SMEM] * 5,
        out_specs=SMEM,
        compiler_params=params(4),
        cost_estimate=pl.CostEstimate(flops=10_000_000, bytes_accessed=10_000, transcendentals=0),
        name="plan",
    )(place, times, active_leaves, active_count, mig_leaf)
    replies = pl.pallas_call(
        reply_kernel,
        out_shape=[shape(4 * IMPORT, LANES)] * SIDES,
        in_specs=[SMEM] * SIDES + [VMEM] * 2,
        out_specs=[VMEM] * SIDES,
        compiler_params=params(4),
        name="replies",
    )(*asked, positions, masses)
    received = [shifted(r, -o) for r, o in zip(replies, OFFSETS)]
    pair_scratch = [pltpu.VMEM((3, LANES, LANES), F32), pltpu.VMEM((3, LANES, LANES), F32)]
    kicks = pl.pallas_call(
        local_kernel,
        out_shape=shape(ACT, 8, LANES),
        in_specs=[SMEM, SMEM, VMEM, VMEM, pl.BlockSpec(memory_space=pl.ANY)],
        out_specs=VMEM,
        scratch_shapes=pair_scratch,
        compiler_params=params(8),
        cost_estimate=pl.CostEstimate(flops=10_000_000, bytes_accessed=10_000, transcendentals=0),
        name="local_pairs",
    )(plan, active_leaves, positions, masses, replies[0])
    imports = [pltpu.VMEM((4 * IMPORTS, LANES), F32)]
    kicks, *blocks = pl.pallas_call(
        leaving_kernel,
        out_shape=[shape(ACT, 8, LANES)] + [shape(7, SLOTS, LANES)] * SIDES,
        in_specs=[SMEM] * 3 + [VMEM] * (4 + SIDES),
        out_specs=[VMEM] * (1 + SIDES),
        scratch_shapes=imports + pair_scratch,
        compiler_params=params(8),
        name="leaving",
    )(plan, active_leaves, mig_leaf, positions, velocities, masses, kicks, *received)
    arrived = [shifted(b, o) for b, o in zip(blocks, OFFSETS)]
    new_positions, new_velocities = pl.pallas_call(
        staying_kernel,
        out_shape=[shape(3, leaves, LANES)] * 2,
        in_specs=[SMEM] * 2 + [VMEM] * (3 + SIDES),
        out_specs=[VMEM] * 2,
        scratch_shapes=[pltpu.VMEM((ACT, 8, LANES), F32)] + imports + pair_scratch,
        compiler_params=params(16),
        cost_estimate=pl.CostEstimate(flops=100_000_000, bytes_accessed=10_000, transcendentals=0),
        name="staying",
    )(plan, active_leaves, positions, velocities, kicks, *received)
    arrived = jnp.concatenate(arrived, axis=1)
    return new_positions, new_velocities, arrived


def solution(mesh):
    return jax.shard_map(
        per_device,
        mesh=mesh,
        in_specs=(
            P(None, "dom", None),
            P(None, "dom", None),
            P("dom", None),
            P("dom"),
            P("dom"),
            P("dom", None),
            P("dom", None),
            P("dom"),
        ),
        out_specs=(P(None, "dom", None), P(None, "dom", None), P(None, "dom", None)),
        check_vma=False,
    )
```

```python
import functools
import math

import jax
import jax.numpy as jnp
from jax import lax
from jax.experimental import pallas as pl
from jax.experimental.pallas import tpu as pltpu
from jax.sharding import PartitionSpec as P

REACH = 2
SLOTS = 4
IMPORT = 8
ACT = 16
PARTNERS = 16
LANES = 128
SIDES = 2 * REACH
IMPORTS = SIDES * IMPORT
BIG = 1 << 20
OFFSETS = [o for o in range(-REACH, REACH + 1) if o != 0]

soften = 0.02
EPS = 4.0 * soften * soften
NEG_LOG2E = -math.log2(math.e)
TWO_OVER_ROOT_PI = 2.0 / math.sqrt(math.pi)

F32, BF16, I32 = jnp.float32, jnp.bfloat16, jnp.int32

CHUNK = 8
AHEAD = 2 * CHUNK
COARSE, ROWS = 16, 48
REMOTE, LOCAL, N_REMOTE, N_LOCAL, PLAN = 0, 304, 608, 609, 616
SLOT_BIT, LEAF_BIT, PLACE_BIT = 22, 13, 5

VMEM = pl.BlockSpec(memory_space=pltpu.VMEM)
SMEM = pl.BlockSpec(memory_space=pltpu.SMEM)
ANY = pl.BlockSpec(memory_space=pl.ANY)


def params(mib):
    return pltpu.CompilerParams(vmem_limit_bytes=mib << 20)


def shifted(shard, by):
    length = lax.axis_size("dom")
    return lax.ppermute(shard, "dom", [(i, (i + by) % length) for i in range(length)])


def request_kernel(domains, me_ref, owner_ref, leaf_ref, *outs):
    requests, map_ref, mult_ref = outs[:SIDES], outs[SIDES], outs[SIDES + 1]
    leaf = leaf_ref[...]
    relative = owner_ref[...] - me_ref[0] + REACH
    relative = jnp.where(relative < 0, relative + domains, relative)
    relative = jnp.where(relative >= domains, relative - domains, relative)
    lane = lax.broadcasted_iota(I32, (1, LANES), 1)
    place = IMPORTS + leaf
    for side, offset in enumerate(OFFSETS):
        mine = relative == offset + REACH
        key = jnp.where(mine, leaf, BIG)
        rank = jnp.zeros_like(leaf)
        row = jnp.zeros((1, LANES), I32)
        for k in range(IMPORT):
            least = jnp.min(jnp.min(key, axis=0, keepdims=True), axis=1, keepdims=True)
            row = jnp.where(lane == k, jnp.broadcast_to(least, row.shape), row)
            here = key == least
            rank = jnp.where(here, k, rank)
            key = jnp.where(here, BIG, key)
        requests[side][...] = jnp.minimum(row, 511)
        place = jnp.where(mine, side * IMPORT + rank, place)
    map_ref[...] = place
    column = lax.broadcasted_iota(I32, place.shape, 1)
    times = jnp.zeros_like(place)
    earlier = jnp.zeros_like(place)
    for k in range(PARTNERS):
        same = (place == place[:, k : k + 1]).astype(I32)
        times = times + same
        earlier = jnp.where(column > k, earlier + same, earlier)
    mult_ref[...] = jnp.where(earlier > 0, 0, times)


def plan_kernel(map_ref, mult_ref, count_ref, plan_ref):
    def one_slot(a, sizes):
        n_remote, n_local = sizes
        for k in range(PARTNERS):
            place, times = map_ref[a, k], mult_ref[a, k]
            word = (a << SLOT_BIT) + times
            plan_ref[REMOTE + AHEAD + n_remote] = word + (place << PLACE_BIT)
            plan_ref[LOCAL + AHEAD + n_local] = word + ((place - IMPORTS) << LEAF_BIT) + (n_local << PLACE_BIT)
            counts = jnp.where(times > 0, 1, 0)
            remote = jnp.where(place < IMPORTS, counts, 0)
            n_remote, n_local = n_remote + remote, n_local + counts - remote
        return n_remote, n_local

    n_remote, n_local = lax.fori_loop(0, count_ref[0], one_slot, (jnp.int32(0), jnp.int32(0)))
    for i in range(AHEAD):
        plan_ref[REMOTE + i] = 0
        plan_ref[LOCAL + i] = 0
    for i in range(3 * CHUNK):
        plan_ref[REMOTE + AHEAD + n_remote + i] = 0
        plan_ref[LOCAL + AHEAD + n_local + i] = 0
    plan_ref[N_REMOTE] = n_remote
    plan_ref[N_LOCAL] = n_local


def reply_kernel(r0, r1, r2, r3, _, positions_ref, masses_ref, o0, o1, o2, o3):
    for request, out in ((r0, o0), (r1, o1), (r2, o2), (r3, o3)):
        for k in range(IMPORT):
            at = pl.ds(request[0, k], 1)
            for c in range(3):
                out[8 * c + k : 8 * c + k + 1, :] = 2.0 * positions_ref[c, at, :]
            out[24 + k : 25 + k, :] = masses_ref[at, :]


def pieces(v):
    a = v.astype(BF16).astype(F32)
    b = (v - a).astype(BF16).astype(F32)
    return a, b, v - a - b


def split_rows(xs):
    h = [jnp.floor(x * 128.0 + 0.5) * (1.0 / 128.0) for x in xs]
    l = [x - y for x, y in zip(xs, h)]
    l1 = [v.astype(BF16).astype(F32) for v in l]
    l2 = [v - w for v, w in zip(l, l1)]
    coarse = h[0] * h[0] + h[1] * h[1] + h[2] * h[2]
    fine = sum(b * (2.0 * a + b) for a, b in zip(h, l))
    return h, l1, l2, coarse, fine


def times_minus_two(rows):
    return [-2.0 * r for r in rows]


def source_rows(xs):
    h, l1, l2, coarse, fine = split_rows(xs)
    one, none = jnp.ones_like(coarse), [None]
    first = times_minus_two(h) + [*pieces(coarse), one, one, one] + none * 7
    return first + [*h, *h, *l1, *l2, *l1, *l1, *l2, *l2, *pieces(fine), one, one, one] + none * 2


def target_rows(xs):
    h, l1, l2, coarse, fine = split_rows(xs)
    one, none = jnp.ones_like(coarse), [None]
    first = h + [one, one, one, *pieces(coarse)] + none * 7
    n1, n2, nh = times_minus_two(l1), times_minus_two(l2), times_minus_two(h)
    return first + [*n1, *n2, *nh, *nh, *n1, *n2, *n1, *n2, one, one, one, *pieces(fine + EPS)] + none * 2


def by_leaf(stage, rows, start=0):
    for r, row in enumerate(rows):
        stage[pl.ds(start + r, 8, stride=len(rows)), :] = jnp.zeros((8, LANES), F32) if row is None else row


def set_sources(first, xs, m, stage, sources, blocks):
    by_leaf(stage, source_rows(xs))
    pad = jnp.zeros((LANES - ROWS, LANES), F32)
    for k in range(8):
        wide = jnp.concatenate([stage[ROWS * k : ROWS * (k + 1), :], pad], axis=0)
        sources[first + k] = jnp.transpose(wide)[:, :ROWS].astype(BF16)
    rows = [*xs, jnp.ones_like(m), m] + [None] * 3
    by_leaf(blocks, rows, start=8 * first)


def run_list(plan_ref, base, n, targets, centers, sources, blocks, sums, square, split):
    square[...] = jnp.ones_like(square)
    split[...] = jnp.zeros_like(split)

    def fields(word):
        return lax.shift_right_logical(word, SLOT_BIT), lax.shift_right_logical(word, PLACE_BIT) & 255

    @pl.loop(0, lax.shift_right_logical(n + CHUNK - 1, 3) + 2)
    def _(q):
        start = base + q * CHUNK
        for t in range(CHUNK):
            word = plan_ref[start + t]
            slot, place = fields(word)
            block = blocks[pl.ds(pl.multiple_of(8 * place, 8), 8), :]
            mass = block[4:5] * (word & 31).astype(F32)
            a, b, c = pieces((block - centers[slot]) * mass)
            weights = jnp.concatenate([a, b, c, jnp.zeros_like(c)], axis=0).astype(BF16)
            out = jnp.dot(jnp.concatenate([weights, weights], axis=1), split[t], preferred_element_type=F32)
            sums[slot] += out[0:8] + out[8:16] + out[16:24]
        for t in range(CHUNK):
            sq = square[t]
            inverse = lax.rsqrt(sq)
            gauss = TWO_OVER_ROOT_PI * jnp.exp2(sq * NEG_LOG2E)
            law = ((1.0 - lax.erf(sq * inverse)) * inverse + gauss) * (inverse * inverse)
            high = law.astype(BF16)
            split[t, :LANES] = high
            split[t, LANES:] = (law - high.astype(F32)).astype(BF16)
        for t in range(CHUNK):
            slot, place = fields(plan_ref[start + AHEAD + t])
            square[t] = jnp.dot(
                sources[place, :, :COARSE], targets[slot, :COARSE], preferred_element_type=F32
            ) + jnp.dot(sources[place, :, COARSE:], targets[slot, COARSE:], preferred_element_type=F32)


def local_kernel(plan_ref, active_ref, positions_ref, masses_ref, _, sums, targets, centers,
                 held, stage, sources, blocks, square, split):
    for a in range(ACT):
        at = pl.ds(active_ref[a], 1)
        for c in range(3):
            held[16 * c + a : 16 * c + a + 1, :] = 2.0 * positions_ref[c, at, :]
    for g in range(ACT // 8):
        xs = [held[16 * c + 8 * g : 16 * c + 8 * g + 8, :] for c in range(3)]
        by_leaf(stage, target_rows(xs))
        for k in range(8):
            targets[8 * g + k] = stage[ROWS * k : ROWS * (k + 1), :].astype(BF16)
        means = [jnp.broadcast_to(jnp.mean(x, axis=1, keepdims=True), x.shape) for x in xs]
        by_leaf(stage, means + [None] * 5)
        for k in range(8):
            centers[8 * g + k] = stage[8 * k : 8 * k + 8, :]
    sums[...] = jnp.zeros_like(sums)
    n = plan_ref[N_LOCAL]

    @pl.when(n > 0)
    def _():
        @pl.loop(0, lax.shift_right_logical(n + 7, 3))
        def _(g):
            for k in range(8):
                word = plan_ref[LOCAL + AHEAD + 8 * g + k]
                at = pl.ds(lax.shift_right_logical(word, LEAF_BIT) & 511, 1)
                for c in range(3):
                    held[8 * c + k : 8 * c + k + 1, :] = 2.0 * positions_ref[c, at, :]
                held[24 + k : 25 + k, :] = masses_ref[at, :]
            xs = [held[8 * c : 8 * c + 8, :] for c in range(3)]
            set_sources(pl.multiple_of(8 * g, 8), xs, held[24:32, :], stage, sources, blocks)

        run_list(plan_ref, LOCAL, n, targets, centers, sources, blocks, sums, square, split)


def remote_kernel(plan_ref, active_ref, count_ref, mig_ref, positions_ref, velocities_ref, masses_ref,
                  sums_in, targets, centers, r0, r1, r2, r3, new_positions, new_velocities, b0, b1, b2, b3,
                  stage, sources, blocks, sums, square, split):
    for side, received in enumerate((r0, r1, r2, r3)):
        xs = [received[8 * c : 8 * c + 8, :] for c in range(3)]
        set_sources(8 * side, xs, received[24:32, :], stage, sources, blocks)
    sums[...] = sums_in[...]
    run_list(plan_ref, REMOTE, plan_ref[N_REMOTE], targets, centers, sources, blocks, sums, square, split)
    new_velocities[...] = velocities_ref[...]
    new_positions[...] = positions_ref[...] + 0.25 * velocities_ref[...]

    @pl.loop(0, count_ref[0])
    def _(a):
        at = pl.ds(active_ref[a], 1)
        total, center = sums[a], centers[a]
        for c in range(3):
            x = positions_ref[c, at, :]
            v = velocities_ref[c, at, :] + (total[c : c + 1] - (2.0 * x - center[c : c + 1]) * total[3:4])
            new_velocities[c, at, :] = v
            new_positions[c, at, :] = x + 0.25 * v

    for side, block in enumerate((b0, b1, b2, b3)):
        for k in range(SLOTS):
            leaf = mig_ref[side * SLOTS + k]
            at = pl.ds(jnp.maximum(leaf, 0), 1)
            held = jnp.full((1, LANES), jnp.where(leaf >= 0, 1, 0), I32) > 0
            for c in range(3):
                block[c, k : k + 1, :] = jnp.where(held, new_positions[c, at, :], 0.0)
                block[3 + c, k : k + 1, :] = jnp.where(held, new_velocities[c, at, :], 0.0)
            block[6, k : k + 1, :] = jnp.where(held, masses_ref[at, :], 0.0)


def shape(*dims, dtype=F32):
    return jax.ShapeDtypeStruct(dims, dtype)


def per_device(positions, velocities, masses, active_leaves, active_count, partner_owner, partner_leaf, mig_leaf):
    leaves = positions.shape[1]
    domains = lax.axis_size("dom")
    me = lax.axis_index("dom").astype(I32).reshape(1)
    *requests, place, times = pl.pallas_call(
        functools.partial(request_kernel, domains),
        out_shape=[shape(1, LANES, dtype=I32)] * SIDES + [shape(ACT, PARTNERS, dtype=I32)] * 2,
        in_specs=[SMEM, VMEM, VMEM],
        out_specs=[VMEM] * (SIDES + 2),
        compiler_params=params(4),
        name="requests",
    )(me, partner_owner, partner_leaf)
    asked = [shifted(r, o) for r, o in zip(requests, OFFSETS)]
    plan = pl.pallas_call(
        plan_kernel,
        out_shape=shape(PLAN, dtype=I32),
        in_specs=[SMEM] * 3,
        out_specs=SMEM,
        compiler_params=params(4),
        cost_estimate=pl.CostEstimate(flops=10_000_000, bytes_accessed=10_000, transcendentals=0),
        name="plan",
    )(place, times, active_count)
    replies = pl.pallas_call(
        reply_kernel,
        out_shape=[shape(4 * IMPORT, LANES)] * SIDES,
        in_specs=[SMEM] * SIDES + [ANY] + [VMEM] * 2,
        out_specs=[VMEM] * SIDES,
        compiler_params=params(4),
        name="replies",
    )(*asked, plan, positions, masses)
    received = [shifted(r, -o) for r, o in zip(replies, OFFSETS)]

    def tables(n):
        return [
            pltpu.VMEM((8 * ROWS, LANES), F32),
            pltpu.VMEM((n, LANES, ROWS), BF16),
            pltpu.VMEM((8 * n, LANES), F32),
        ]

    chunks = [pltpu.VMEM((CHUNK, LANES, LANES), F32), pltpu.VMEM((CHUNK, 2 * LANES, LANES), BF16)]
    sums = shape(ACT, 8, LANES)
    sums, targets, centers = pl.pallas_call(
        local_kernel,
        out_shape=[sums, shape(ACT, ROWS, LANES, dtype=BF16), sums],
        in_specs=[SMEM, SMEM, VMEM, VMEM, ANY],
        out_specs=[VMEM] * 3,
        scratch_shapes=[pltpu.VMEM((48, LANES), F32)] + tables(ACT * PARTNERS) + chunks,
        compiler_params=params(24),
        cost_estimate=pl.CostEstimate(flops=10_000_000, bytes_accessed=10_000, transcendentals=0),
        name="local_pairs",
    )(plan, active_leaves, positions, masses, replies[0])
    new_positions, new_velocities, *blocks = pl.pallas_call(
        remote_kernel,
        out_shape=[shape(3, leaves, LANES)] * 2 + [shape(7, SLOTS, LANES)] * SIDES,
        in_specs=[SMEM] * 4 + [VMEM] * (6 + SIDES),
        out_specs=[VMEM] * (2 + SIDES),
        scratch_shapes=tables(IMPORTS) + [pltpu.VMEM((ACT, 8, LANES), F32)] + chunks,
        compiler_params=params(16),
        cost_estimate=pl.CostEstimate(flops=100_000_000, bytes_accessed=10_000, transcendentals=0),
        name="remote_pairs",
    )(plan, active_leaves, active_count, mig_leaf, positions, velocities, masses, sums, targets, centers, *received)
    arrived = [shifted(b, o) for b, o in zip(blocks, OFFSETS)]
    arrived = jnp.concatenate(arrived, axis=1)
    return new_positions, new_velocities, arrived


def solution(mesh):
    return jax.shard_map(
        per_device,
        mesh=mesh,
        in_specs=(
            P(None, "dom", None),
            P(None, "dom", None),
            P("dom", None),
            P("dom"),
            P("dom"),
            P("dom", None),
            P("dom", None),
            P("dom"),
        ),
        out_specs=(P(None, "dom", None), P(None, "dom", None), P(None, "dom", None)),
        check_vma=False,
    )
```

```python
import functools
import math

import jax
import jax.numpy as jnp
from jax import lax
from jax.experimental import pallas as pl
from jax.experimental.pallas import tpu as pltpu
from jax.sharding import PartitionSpec as P

REACH = 2
SLOTS = 4
IMPORT = 8
ACT = 16
PARTNERS = 16
LANES = 128
SIDES = 2 * REACH
IMPORTS = SIDES * IMPORT
BIG = 1 << 20

soften = 0.02
EPS = 4.0 * soften * soften
NEG_LOG2E = -math.log2(math.e)
TWO_OVER_ROOT_PI = 2.0 / math.sqrt(math.pi)

F32, BF16, I32 = jnp.float32, jnp.bfloat16, jnp.int32

CHUNK = 8
AHEAD = 2 * CHUNK
COARSE, ROWS = 16, 48
LEAVING, STAYING, LOCAL, SIZES, LIVE, ACTIVE, MIG, FROM, PLAN = 0, 304, 608, 912, 915, 920, 936, 952, 968
SLOT_BIT, LEAF_BIT, PLACE_BIT = 22, 13, 5

VMEM = pl.BlockSpec(memory_space=pltpu.VMEM)
SMEM = pl.BlockSpec(memory_space=pltpu.SMEM)
ANY = pl.BlockSpec(memory_space=pl.ANY)
HBM = pl.BlockSpec(memory_space=pltpu.HBM)


def params(mib):
    return pltpu.CompilerParams(vmem_limit_bytes=mib << 20)


def swapped(shard, partner):
    return lax.ppermute(shard, "dom", [(i, partner(i) % lax.axis_size("dom")) for i in range(lax.axis_size("dom"))])


PARTNERS_OF = (
    lambda d: d + 2 if d & 2 else d - 2,
    lambda d: d + 1 if d & 1 else d - 1,
    lambda d: d ^ 2,
    lambda d: d ^ 1,
)


def swap_offsets(me):
    one, two = 1 - 2 * (me & 1), 2 - 2 * (me & 2)
    return -two, -one, two, one


def request_kernel(domains, me_ref, owner_hbm, leaf_hbm, *outs):
    requests, (map_ref, mult_ref, owner_ref, leaf_ref, owner_sem, leaf_sem) = outs[:SIDES], outs[SIDES:]
    copies = [
        pltpu.make_async_copy(owner_hbm, owner_ref, owner_sem),
        pltpu.make_async_copy(leaf_hbm, leaf_ref, leaf_sem),
    ]
    for copy in copies:
        copy.start()
    for copy in copies:
        copy.wait()
    leaf = leaf_ref[...]
    relative = owner_ref[...] - me_ref[0] + REACH
    relative = jnp.where(relative < 0, relative + domains, relative)
    relative = jnp.where(relative >= domains, relative - domains, relative)
    lane = lax.broadcasted_iota(I32, (1, LANES), 1)
    place = IMPORTS + leaf
    for side, offset in enumerate(swap_offsets(me_ref[0])):
        mine = relative == offset + REACH
        key = jnp.where(mine, leaf, BIG)
        rank = jnp.zeros_like(leaf)
        row = jnp.zeros((1, LANES), I32)
        for k in range(IMPORT):
            least = jnp.min(jnp.min(key, axis=0, keepdims=True), axis=1, keepdims=True)
            row = jnp.where(lane == k, jnp.broadcast_to(least, row.shape), row)
            here = key == least
            rank = jnp.where(here, k, rank)
            key = jnp.where(here, BIG, key)
        requests[side][...] = jnp.minimum(row, 511)
        place = jnp.where(mine, side * IMPORT + rank, place)
    map_ref[...] = place
    column = lax.broadcasted_iota(I32, place.shape, 1)
    times = jnp.zeros_like(place)
    earlier = jnp.zeros_like(place)
    for k in range(PARTNERS):
        same = (place == place[:, k : k + 1]).astype(I32)
        times = times + same
        earlier = jnp.where(column > k, earlier + same, earlier)
    mult_ref[...] = jnp.where(earlier > 0, 0, times)


def plan_kernel(map_ref, mult_ref, count_ref, active_ref, mig_ref, positions_hbm, masses_hbm,
                plan_ref, points, positions_sem, masses_sem):
    copies = [
        pltpu.make_async_copy(positions_hbm, points.at[:3], positions_sem),
        pltpu.make_async_copy(masses_hbm, points.at[3], masses_sem),
    ]
    for copy in copies:
        copy.start()
    live = count_ref[0]
    plan_ref[LIVE] = live
    for n in range(SIDES * SLOTS):
        plan_ref[MIG + n] = mig_ref[n]
        plan_ref[FROM + n] = -1
    for a in range(ACT):
        plan_ref[ACTIVE + a] = active_ref[a]

    def one_slot(a, ends):
        leaving_end, staying_end, n_local = ends
        leaf = active_ref[a]
        hits = jnp.int32(0)
        for n in range(SIDES * SLOTS):
            hit = mig_ref[n] == leaf
            plan_ref[FROM + n] = jnp.where(hit, a, plan_ref[FROM + n])
            hits = hits + jnp.where(hit, 1, 0)
        end = jnp.where(hits > 0, leaving_end, staying_end)
        for k in range(PARTNERS):
            place, times = map_ref[a, k], mult_ref[a, k]
            word = (a << SLOT_BIT) + times
            plan_ref[end] = word + (place << PLACE_BIT)
            plan_ref[LOCAL + AHEAD + n_local] = word + ((place - IMPORTS) << LEAF_BIT) + (n_local << PLACE_BIT)
            counts = jnp.where(times > 0, 1, 0)
            remote = jnp.where(place < IMPORTS, counts, 0)
            end, n_local = end + remote, n_local + counts - remote
        return jnp.where(hits > 0, end, leaving_end), jnp.where(hits > 0, staying_end, end), n_local

    starts = (jnp.int32(LEAVING + AHEAD), jnp.int32(STAYING + AHEAD), jnp.int32(0))
    leaving_end, staying_end, n_local = lax.fori_loop(0, live, one_slot, starts)
    for i in range(AHEAD):
        plan_ref[LEAVING + i] = 0
        plan_ref[STAYING + i] = 0
        plan_ref[LOCAL + i] = 0
    for i in range(3 * CHUNK):
        plan_ref[leaving_end + i] = 0
        plan_ref[staying_end + i] = 0
        plan_ref[LOCAL + AHEAD + n_local + i] = 0
    plan_ref[SIZES] = leaving_end - (LEAVING + AHEAD)
    plan_ref[SIZES + 1] = staying_end - (STAYING + AHEAD)
    plan_ref[SIZES + 2] = n_local
    for copy in copies:
        copy.wait()


def reply_kernel(r0, r1, r2, r3, _, points, o0, o1, o2, o3):
    for request, out in ((r0, o0), (r1, o1), (r2, o2), (r3, o3)):
        for k in range(IMPORT):
            at = pl.ds(request[0, k], 1)
            for c in range(3):
                out[8 * c + k : 8 * c + k + 1, :] = 2.0 * points[c, at, :]
            out[24 + k : 25 + k, :] = points[3, at, :]


def pieces(v):
    a = v.astype(BF16).astype(F32)
    b = (v - a).astype(BF16).astype(F32)
    return a, b, v - a - b


def split_rows(xs):
    h = [jnp.floor(x * 128.0 + 0.5) * (1.0 / 128.0) for x in xs]
    l = [x - y for x, y in zip(xs, h)]
    l1 = [v.astype(BF16).astype(F32) for v in l]
    l2 = [v - w for v, w in zip(l, l1)]
    coarse = h[0] * h[0] + h[1] * h[1] + h[2] * h[2]
    fine = sum(b * (2.0 * a + b) for a, b in zip(h, l))
    return h, l1, l2, coarse, fine


def times_minus_two(rows):
    return [-2.0 * r for r in rows]


def source_rows(xs):
    h, l1, l2, coarse, fine = split_rows(xs)
    one, none = jnp.ones_like(coarse), [None]
    first = times_minus_two(h) + [*pieces(coarse), one, one, one] + none * 7
    return first + [*h, *h, *l1, *l2, *l1, *l1, *l2, *l2, *pieces(fine), one, one, one] + none * 2


def target_rows(xs):
    h, l1, l2, coarse, fine = split_rows(xs)
    one, none = jnp.ones_like(coarse), [None]
    first = h + [one, one, one, *pieces(coarse)] + none * 7
    n1, n2, nh = times_minus_two(l1), times_minus_two(l2), times_minus_two(h)
    return first + [*n1, *n2, *nh, *nh, *n1, *n2, *n1, *n2, one, one, one, *pieces(fine + EPS)] + none * 2


def by_leaf(stage, rows, start=0):
    for r, row in enumerate(rows):
        stage[pl.ds(start + r, 8, stride=len(rows)), :] = jnp.zeros((8, LANES), F32) if row is None else row


def set_sources(first, xs, m, stage, sources, blocks):
    by_leaf(stage, source_rows(xs))
    pad = jnp.zeros((LANES - ROWS, LANES), F32)
    for k in range(8):
        wide = jnp.concatenate([stage[ROWS * k : ROWS * (k + 1), :], pad], axis=0)
        sources[first + k] = jnp.transpose(wide)[:, :ROWS].astype(BF16)
    rows = [*xs, jnp.ones_like(m), m] + [None] * 3
    by_leaf(blocks, rows, start=8 * first)


def run_list(plan_ref, base, n, targets, centers, sources, blocks, sums, square, split):
    square[...] = jnp.ones_like(square)
    split[...] = jnp.zeros_like(split)

    def fields(word):
        return lax.shift_right_logical(word, SLOT_BIT), lax.shift_right_logical(word, PLACE_BIT) & 255

    @pl.loop(0, lax.shift_right_logical(n + CHUNK - 1, 3) + 2)
    def _(q):
        start = base + q * CHUNK
        for t in range(CHUNK):
            word = plan_ref[start + t]
            slot, place = fields(word)
            block = blocks[pl.ds(pl.multiple_of(8 * place, 8), 8), :]
            mass = block[4:5] * (word & 31).astype(F32)
            a, b, c = pieces((block - centers[slot]) * mass)
            weights = jnp.concatenate([a, b, c, jnp.zeros_like(c)], axis=0).astype(BF16)
            out = jnp.dot(jnp.concatenate([weights, weights], axis=1), split[t], preferred_element_type=F32)
            sums[slot] += out[0:8] + out[8:16] + out[16:24]
        for t in range(CHUNK):
            sq = square[t]
            inverse = lax.rsqrt(sq)
            gauss = TWO_OVER_ROOT_PI * jnp.exp2(sq * NEG_LOG2E)
            law = ((1.0 - lax.erf(sq * inverse)) * inverse + gauss) * (inverse * inverse)
            high = law.astype(BF16)
            split[t, :LANES] = high
            split[t, LANES:] = (law - high.astype(F32)).astype(BF16)
        for t in range(CHUNK):
            slot, place = fields(plan_ref[start + AHEAD + t])
            square[t] = jnp.dot(
                sources[place, :, :COARSE], targets[slot, :COARSE], preferred_element_type=F32
            ) + jnp.dot(sources[place, :, COARSE:], targets[slot, COARSE:], preferred_element_type=F32)


def local_kernel(plan_ref, points, _, sums, targets, centers, held, stage, sources, blocks, square, split):
    for a in range(ACT):
        at = pl.ds(plan_ref[ACTIVE + a], 1)
        for c in range(3):
            held[16 * c + a : 16 * c + a + 1, :] = 2.0 * points[c, at, :]
    for g in range(ACT // 8):
        xs = [held[16 * c + 8 * g : 16 * c + 8 * g + 8, :] for c in range(3)]
        by_leaf(stage, target_rows(xs))
        for k in range(8):
            targets[8 * g + k] = stage[ROWS * k : ROWS * (k + 1), :].astype(BF16)
        means = [jnp.broadcast_to(jnp.mean(x, axis=1, keepdims=True), x.shape) for x in xs]
        by_leaf(stage, means + [None] * 5)
        for k in range(8):
            centers[8 * g + k] = stage[8 * k : 8 * k + 8, :]
    sums[...] = jnp.zeros_like(sums)
    n = plan_ref[SIZES + 2]

    @pl.when(n > 0)
    def _():
        @pl.loop(0, lax.shift_right_logical(n + 7, 3))
        def _(g):
            for k in range(8):
                word = plan_ref[LOCAL + AHEAD + 8 * g + k]
                at = pl.ds(lax.shift_right_logical(word, LEAF_BIT) & 511, 1)
                for c in range(3):
                    held[8 * c + k : 8 * c + k + 1, :] = 2.0 * points[c, at, :]
                held[24 + k : 25 + k, :] = points[3, at, :]
            xs = [held[8 * c : 8 * c + 8, :] for c in range(3)]
            set_sources(pl.multiple_of(8 * g, 8), xs, held[24:32, :], stage, sources, blocks)

        run_list(plan_ref, LOCAL, n, targets, centers, sources, blocks, sums, square, split)


def kicked(x, v, total, center, c):
    return v + (total[c : c + 1] - (2.0 * x - center[c : c + 1]) * total[3:4])


def leaving_kernel(me_ref, plan_ref, points, velocities_ref, sums_in, targets, centers, r0, r1, r2, r3,
                   sums, sources, blocks, b0, b1, b2, b3, stage, square, split):
    for side, received in enumerate((r0, r1, r2, r3)):
        xs = [received[8 * c : 8 * c + 8, :] for c in range(3)]
        set_sources(8 * side, xs, received[24:32, :], stage, sources, blocks)
    sums[...] = sums_in[...]
    n_leaving = plan_ref[SIZES]

    @pl.when(n_leaving > 0)
    def _():
        run_list(plan_ref, LEAVING, n_leaving, targets, centers, sources, blocks, sums, square, split)

    for offset, block in zip(swap_offsets(me_ref[0]), (b0, b1, b2, b3)):
        number = SLOTS * (offset + jnp.where(offset < 0, REACH, REACH - 1))
        for k in range(SLOTS):
            leaf, a = plan_ref[MIG + number + k], plan_ref[FROM + number + k]
            at = pl.ds(jnp.maximum(leaf, 0), 1)
            held = jnp.full((1, LANES), jnp.where(leaf >= 0, 1, 0), I32) > 0
            live = jnp.full((1, LANES), jnp.where(a >= 0, 1, 0), I32) > 0
            total, center = sums[jnp.maximum(a, 0)], centers[jnp.maximum(a, 0)]
            for c in range(3):
                x, v = points[c, at, :], velocities_ref[c, at, :]
                v = jnp.where(live, kicked(x, v, total, center, c), v)
                block[c, k : k + 1, :] = jnp.where(held, x + 0.25 * v, 0.0)
                block[3 + c, k : k + 1, :] = jnp.where(held, v, 0.0)
            block[6, k : k + 1, :] = jnp.where(held, points[3, at, :], 0.0)


def staying_kernel(plan_ref, points, velocities_ref, sums_in, targets, centers, sources, blocks,
                   new_positions, new_velocities, sums, square, split):
    sums[...] = sums_in[...]
    new_velocities[...] = velocities_ref[...]
    new_positions[...] = points[:3] + 0.25 * velocities_ref[...]
    run_list(plan_ref, STAYING, plan_ref[SIZES + 1], targets, centers, sources, blocks, sums, square, split)

    @pl.loop(0, plan_ref[LIVE])
    def _(a):
        at = pl.ds(plan_ref[ACTIVE + a], 1)
        total, center = sums[a], centers[a]
        for c in range(3):
            x = points[c, at, :]
            v = kicked(x, velocities_ref[c, at, :], total, center, c)
            new_velocities[c, at, :] = v
            new_positions[c, at, :] = x + 0.25 * v


def shape(*dims, dtype=F32):
    return jax.ShapeDtypeStruct(dims, dtype)


def per_device(positions, velocities, masses, active_leaves, active_count, partner_owner, partner_leaf, mig_leaf):
    leaves = positions.shape[1]
    domains = lax.axis_size("dom")
    me = lax.axis_index("dom").astype(I32)
    dma = pltpu.SemaphoreType.DMA
    entries = shape(ACT, PARTNERS, dtype=I32)
    *requests, place, times = pl.pallas_call(
        functools.partial(request_kernel, domains),
        out_shape=[shape(1, LANES, dtype=I32)] * SIDES + [entries] * 2,
        in_specs=[SMEM, HBM, HBM],
        out_specs=[VMEM] * (SIDES + 2),
        scratch_shapes=[pltpu.VMEM((ACT, PARTNERS), I32)] * 2 + [dma] * 2,
        compiler_params=params(4),
        name="requests",
    )(me.reshape(1), partner_owner, partner_leaf)
    asked = [swapped(r, p) for r, p in zip(requests, PARTNERS_OF)]
    plan, points = pl.pallas_call(
        plan_kernel,
        out_shape=[shape(PLAN, dtype=I32), shape(4, leaves, LANES)],
        in_specs=[SMEM] * 5 + [HBM] * 2,
        out_specs=[SMEM, VMEM],
        scratch_shapes=[dma] * 2,
        compiler_params=params(4),
        cost_estimate=pl.CostEstimate(flops=10_000_000, bytes_accessed=10_000, transcendentals=0),
        name="plan",
    )(place, times, active_count, active_leaves, mig_leaf, positions, masses)
    replies = pl.pallas_call(
        reply_kernel,
        out_shape=[shape(4 * IMPORT, LANES)] * SIDES,
        in_specs=[SMEM] * SIDES + [ANY, VMEM],
        out_specs=[VMEM] * SIDES,
        compiler_params=params(4),
        name="replies",
    )(*asked, plan, points)
    received = [swapped(r, p) for r, p in zip(replies, PARTNERS_OF)]
    stage = [pltpu.VMEM((8 * ROWS, LANES), F32)]
    chunks = [pltpu.VMEM((CHUNK, LANES, LANES), F32), pltpu.VMEM((CHUNK, 2 * LANES, LANES), BF16)]
    slot_sums, all_own = shape(ACT, 8, LANES), ACT * PARTNERS
    sums, targets, centers = pl.pallas_call(
        local_kernel,
        out_shape=[slot_sums, shape(ACT, ROWS, LANES, dtype=BF16), slot_sums],
        in_specs=[SMEM, VMEM, ANY],
        out_specs=[VMEM] * 3,
        scratch_shapes=[pltpu.VMEM((48, LANES), F32)]
        + stage
        + [pltpu.VMEM((all_own, LANES, ROWS), BF16), pltpu.VMEM((8 * all_own, LANES), F32)]
        + chunks,
        compiler_params=params(24),
        cost_estimate=pl.CostEstimate(flops=10_000_000, bytes_accessed=10_000, transcendentals=0),
        name="local_pairs",
    )(plan, points, replies[0])
    sums, sources, tables, *blocks = pl.pallas_call(
        leaving_kernel,
        out_shape=[slot_sums, shape(IMPORTS, LANES, ROWS, dtype=BF16), shape(8 * IMPORTS, LANES)]
        + [shape(7, SLOTS, LANES)] * SIDES,
        in_specs=[SMEM] * 2 + [VMEM] * (5 + SIDES),
        out_specs=[VMEM] * (3 + SIDES),
        scratch_shapes=stage + chunks,
        compiler_params=params(16),
        name="leaving",
    )(me.reshape(1), plan, points, velocities, sums, targets, centers, *received)
    came = [swapped(b, p) for b, p in zip(blocks, PARTNERS_OF)]
    new_positions, new_velocities = pl.pallas_call(
        staying_kernel,
        out_shape=[shape(3, leaves, LANES)] * 2,
        in_specs=[SMEM] + [VMEM] * 7,
        out_specs=[VMEM] * 2,
        scratch_shapes=[pltpu.VMEM((ACT, 8, LANES), F32)] + chunks,
        compiler_params=params(16),
        cost_estimate=pl.CostEstimate(flops=100_000_000, bytes_accessed=10_000, transcendentals=0),
        name="staying",
    )(plan, points, velocities, sums, targets, centers, sources, tables)
    first_two, even = (me & 2) == 0, (me & 1) == 0
    arrived = jnp.concatenate(
        [
            jnp.where(first_two, came[2], came[0]),
            jnp.where(even, came[3], came[1]),
            jnp.where(even, came[1], came[3]),
            jnp.where(first_two, came[0], came[2]),
        ],
        axis=1,
    )
    return new_positions, new_velocities, arrived


def solution(mesh):
    return jax.shard_map(
        per_device,
        mesh=mesh,
        in_specs=(
            P(None, "dom", None),
            P(None, "dom", None),
            P("dom", None),
            P("dom"),
            P("dom"),
            P("dom", None),
            P("dom", None),
            P("dom"),
        ),
        out_specs=(P(None, "dom", None), P(None, "dom", None), P(None, "dom", None)),
        check_vma=False,
    )
```

```python
import functools
import math

import jax
import jax.numpy as jnp
from jax import lax
from jax.experimental import pallas as pl
from jax.experimental.pallas import tpu as pltpu
from jax.sharding import PartitionSpec as P

REACH = 2
SLOTS = 4
IMPORT = 8
ACT = 16
PARTNERS = 16
LANES = 128
SIDES = 2 * REACH
IMPORTS = SIDES * IMPORT
BIG = 1 << 20
OWNER_BIT = 10
OWNER = 1 << OWNER_BIT

soften = 0.02
EPS = 4.0 * soften * soften
NEG_LOG2E = -math.log2(math.e)
TWO_OVER_ROOT_PI = 2.0 / math.sqrt(math.pi)

F32, BF16, I32 = jnp.float32, jnp.bfloat16, jnp.int32

CHUNK = 8
AHEAD = 2 * CHUNK
COARSE, ROWS = 16, 48
LEAVING, STAYING, LOCAL, SIZES, LIVE, ACTIVE, MIG, FROM, PLAN = 0, 304, 608, 912, 915, 920, 936, 952, 968
SLOT_BIT, PLACE_BIT = 16, 5

VMEM = pl.BlockSpec(memory_space=pltpu.VMEM)
SMEM = pl.BlockSpec(memory_space=pltpu.SMEM)
ANY = pl.BlockSpec(memory_space=pl.ANY)


def params(mib):
    return pltpu.CompilerParams(vmem_limit_bytes=mib << 20)


def swapped(shard, partner):
    return lax.ppermute(shard, "dom", [(i, partner(i) % lax.axis_size("dom")) for i in range(lax.axis_size("dom"))])


PARTNERS_OF = (
    lambda d: d + 2 if d & 2 else d - 2,
    lambda d: d + 1 if d & 1 else d - 1,
    lambda d: d ^ 2,
    lambda d: d ^ 1,
)


def swap_offsets(me):
    one, two = 1 - 2 * (me & 1), 2 - 2 * (me & 2)
    return -two, -one, two, one


def near_first(swaps):
    return [*swaps[2:], *swaps[:2]]


def number_of(offset):
    return offset + jnp.where(offset < 0, REACH, REACH - 1)


def request_kernel(domains, leaves, me_ref, entry_ref, *outs):
    requests, place_ref = outs[:SIDES], outs[SIDES]
    entry = entry_ref[...]
    leaf = entry & (OWNER - 1)
    relative = lax.shift_right_logical(entry, OWNER_BIT) - me_ref[0] + REACH
    relative = jnp.where(relative < 0, relative + domains, relative)
    relative = jnp.where(relative >= domains, relative - domains, relative)
    lane = lax.broadcasted_iota(I32, (1, LANES), 1)
    place = IMPORTS + leaf

    def over_all(reduce, v):
        return reduce(reduce(v, axis=0, keepdims=True), axis=1, keepdims=True)

    for side, offset in enumerate(swap_offsets(me_ref[0])):
        mine = relative == offset + REACH
        low, high = jnp.where(mine, leaf, BIG), jnp.where(mine, leaf, -1)
        rank = jnp.zeros_like(leaf)
        row = jnp.zeros((1, LANES), I32)
        for k in range(IMPORT // 2):
            last = IMPORT - 1 - k
            least, most = over_all(jnp.min, low), over_all(jnp.max, high)
            row = jnp.where(lane == k, jnp.broadcast_to(least, row.shape), row)
            row = jnp.where(lane == last, jnp.broadcast_to(most, row.shape), row)
            rank = jnp.where(low == least, k, jnp.where(high == most, last, rank))
            low = jnp.where(low == least, BIG, low)
            high = jnp.where(high == most, -1, high)
        requests[side][...] = jnp.clip(row, 0, leaves - 1)
        place = jnp.where(mine, side * IMPORT + rank, place)
    place_ref[...] = place


def plan_kernel(place_ref, count_ref, active_ref, mig_ref, _, plan_ref, packed_vector, packed_ref, sem):
    place = place_ref[...]
    column = lax.broadcasted_iota(I32, place.shape, 1)
    times = jnp.zeros_like(place)
    earlier = jnp.zeros_like(place)
    for k in range(PARTNERS):
        same = (place == place[:, k : k + 1]).astype(I32)
        times = times + same
        earlier = jnp.where(column > k, earlier + same, earlier)
    packed_vector[...] = (place << PLACE_BIT) + jnp.where(earlier > 0, 0, times)
    copy = pltpu.make_async_copy(packed_vector, packed_ref, sem)
    copy.start()
    live = count_ref[0]
    plan_ref[LIVE] = live
    for n in range(SIDES * SLOTS):
        plan_ref[MIG + n] = mig_ref[n]
    for a in range(ACT):
        plan_ref[ACTIVE + a] = active_ref[a]
    copy.wait()

    def one_slot(a, carried):
        leaving_end, staying_end, local_end, origins = carried
        leaf = active_ref[a]
        hits = jnp.int32(0)
        found = []
        for n in range(SIDES * SLOTS):
            hit = mig_ref[n] == leaf
            found.append(jnp.where(hit, a, origins[n]))
            hits = hits + jnp.where(hit, 1, 0)
        end = jnp.where(hits > 0, leaving_end, staying_end)
        for k in range(PARTNERS):
            packed = packed_ref[a, k]
            word = (a << SLOT_BIT) + packed
            plan_ref[end] = word
            plan_ref[local_end] = word
            counts = jnp.where((packed & 31) > 0, 1, 0)
            remote = jnp.where(packed < (IMPORTS << PLACE_BIT), counts, 0)
            end, local_end = end + remote, local_end + counts - remote
        leaving_end, staying_end = jnp.where(hits > 0, end, leaving_end), jnp.where(hits > 0, staying_end, end)
        return leaving_end, staying_end, local_end, tuple(found)

    ends = [jnp.int32(base + AHEAD) for base in (LEAVING, STAYING, LOCAL)]
    nowhere = tuple(jnp.int32(-1) for _ in range(SIDES * SLOTS))
    *ends, origins = lax.fori_loop(0, live, one_slot, (*ends, nowhere))
    for n, a in enumerate(origins):
        plan_ref[FROM + n] = a
    for i, (base, end) in enumerate(zip((LEAVING, STAYING, LOCAL), ends)):
        for k in range(AHEAD):
            plan_ref[base + k] = 0
        for k in range(3 * CHUNK):
            plan_ref[end + k] = 0
        plan_ref[SIZES + i] = end - (base + AHEAD)


def reply_kernel(r0, r1, r2, r3, points, o0, o1, o2, o3, token):
    token[...] = jnp.zeros_like(token)
    for request, out in ((r0, o0), (r1, o1), (r2, o2), (r3, o3)):
        for k in range(IMPORT):
            at = pl.ds(request[0, k], 1)
            for c in range(3):
                out[8 * c + k : 8 * c + k + 1, :] = 2.0 * points[c, at, :]
            out[24 + k : 25 + k, :] = points[3, at, :]


def pieces(v):
    a = v.astype(BF16).astype(F32)
    b = (v - a).astype(BF16).astype(F32)
    return a, b, v - a - b


def split_rows(xs):
    h = [jnp.floor(x * 128.0 + 0.5) * (1.0 / 128.0) for x in xs]
    l = [x - y for x, y in zip(xs, h)]
    l1 = [v.astype(BF16).astype(F32) for v in l]
    l2 = [v - w for v, w in zip(l, l1)]
    coarse = h[0] * h[0] + h[1] * h[1] + h[2] * h[2]
    fine = sum(b * (2.0 * a + b) for a, b in zip(h, l))
    return h, l1, l2, coarse, fine


def times_minus_two(rows):
    return [-2.0 * r for r in rows]


def source_rows(xs):
    h, l1, l2, coarse, fine = split_rows(xs)
    one, none = jnp.ones_like(coarse), [None]
    first = times_minus_two(h) + [*pieces(coarse), one, one, one] + none * 7
    return first + [*h, *h, *l1, *l2, *l1, *l1, *l2, *l2, *pieces(fine), one, one, one] + none * 2


def target_rows(xs):
    h, l1, l2, coarse, fine = split_rows(xs)
    one, none = jnp.ones_like(coarse), [None]
    first = h + [one, one, one, *pieces(coarse)] + none * 7
    n1, n2, nh = times_minus_two(l1), times_minus_two(l2), times_minus_two(h)
    return first + [*n1, *n2, *nh, *nh, *n1, *n2, *n1, *n2, one, one, one, *pieces(fine + EPS)] + none * 2


def by_leaf(stage, rows, start=0):
    for r, row in enumerate(rows):
        stage[pl.ds(start + r, 8, stride=len(rows)), :] = jnp.zeros((8, LANES), F32) if row is None else row


def set_sources(first, xs, m, stage, sources, blocks):
    by_leaf(stage, source_rows(xs))
    pad = jnp.zeros((LANES - ROWS, LANES), F32)
    for k in range(8):
        wide = jnp.concatenate([stage[ROWS * k : ROWS * (k + 1), :], pad], axis=0)
        sources[first + k] = jnp.transpose(wide)[:, :ROWS].astype(BF16)
    rows = [*xs, jnp.ones_like(m), m] + [None] * 3
    by_leaf(blocks, rows, start=8 * first)


def run_list(plan_ref, base, n, targets, centers, sources, blocks, sums, square, split, by_position=False):
    square[...] = jnp.ones_like(square)
    split[...] = jnp.zeros_like(split)

    def fields(word, position):
        place = jnp.clip(position, 0, n - 1) if by_position else lax.shift_right_logical(word, PLACE_BIT) & 1023
        return lax.shift_right_logical(word, SLOT_BIT), place

    @pl.loop(0, lax.shift_right_logical(n + CHUNK - 1, 3) + 2)
    def _(q):
        start = base + q * CHUNK
        for t in range(CHUNK):
            word = plan_ref[start + t]
            slot, place = fields(word, q * CHUNK + t - AHEAD)
            block = blocks[pl.ds(pl.multiple_of(8 * place, 8), 8), :]
            mass = block[4:5] * (word & 31).astype(F32)
            a, b, c = pieces((block - centers[slot]) * mass)
            weights = jnp.concatenate([a, b, c, jnp.zeros_like(c)], axis=0).astype(BF16)
            out = jnp.dot(jnp.concatenate([weights, weights], axis=1), split[t], preferred_element_type=F32)
            sums[slot] += out[0:8] + out[8:16] + out[16:24]
        for t in range(CHUNK):
            sq = square[t]
            inverse = lax.rsqrt(sq)
            gauss = TWO_OVER_ROOT_PI * jnp.exp2(sq * NEG_LOG2E)
            law = ((1.0 - lax.erf(sq * inverse)) * inverse + gauss) * (inverse * inverse)
            high = law.astype(BF16)
            split[t, :LANES] = high
            split[t, LANES:] = (law - high.astype(F32)).astype(BF16)
        for t in range(CHUNK):
            slot, place = fields(plan_ref[start + AHEAD + t], q * CHUNK + t)
            square[t] = jnp.dot(
                sources[place, :, :COARSE], targets[slot, :COARSE], preferred_element_type=F32
            ) + jnp.dot(sources[place, :, COARSE:], targets[slot, COARSE:], preferred_element_type=F32)


def stage_kernel(active_ref, positions_ref, masses_ref, _, points, targets, centers, held, stage):
    points[:3] = positions_ref[...]
    points[3] = masses_ref[...]
    for a in range(ACT):
        at = pl.ds(active_ref[a], 1)
        for c in range(3):
            held[16 * c + a : 16 * c + a + 1, :] = 2.0 * positions_ref[c, at, :]
    for g in range(ACT // 8):
        xs = [held[16 * c + 8 * g : 16 * c + 8 * g + 8, :] for c in range(3)]
        by_leaf(stage, target_rows(xs))
        for k in range(8):
            targets[8 * g + k] = stage[ROWS * k : ROWS * (k + 1), :].astype(BF16)
        means = [jnp.broadcast_to(jnp.mean(x, axis=1, keepdims=True), x.shape) for x in xs]
        by_leaf(stage, means + [None] * 5)
        for k in range(8):
            centers[8 * g + k] = stage[8 * k : 8 * k + 8, :]


def local_kernel(plan_ref, points, targets, centers, sums, held, stage, sources, blocks, square, split):
    sums[...] = jnp.zeros_like(sums)
    n = plan_ref[SIZES + 2]

    @pl.when(n > 0)
    def _():
        @pl.loop(0, lax.shift_right_logical(n + 7, 3))
        def _(g):
            for k in range(8):
                word = plan_ref[LOCAL + AHEAD + 8 * g + k]
                leaf = (lax.shift_right_logical(word, PLACE_BIT) & 1023) - IMPORTS
                at = pl.ds(jnp.maximum(leaf, 0), 1)
                for c in range(3):
                    held[8 * c + k : 8 * c + k + 1, :] = 2.0 * points[c, at, :]
                held[24 + k : 25 + k, :] = points[3, at, :]
            xs = [held[8 * c : 8 * c + 8, :] for c in range(3)]
            set_sources(pl.multiple_of(8 * g, 8), xs, held[24:32, :], stage, sources, blocks)

        run_list(plan_ref, LOCAL, n, targets, centers, sources, blocks, sums, square, split, by_position=True)


def kicked(x, v, total, center, c):
    return v + (total[c : c + 1] - (2.0 * x - center[c : c + 1]) * total[3:4])


def leaving_kernel(me_ref, plan_ref, points, velocities_ref, sums_in, targets, centers, r0, r1, r2, r3,
                   sums, sources, blocks, b0, b1, b2, b3, stage, square, split):
    for side, received in enumerate((r0, r1, r2, r3)):
        xs = [received[8 * c : 8 * c + 8, :] for c in range(3)]
        set_sources(8 * side, xs, received[24:32, :], stage, sources, blocks)
    sums[...] = sums_in[...]
    n_leaving = plan_ref[SIZES]

    @pl.when(n_leaving > 0)
    def _():
        run_list(plan_ref, LEAVING, n_leaving, targets, centers, sources, blocks, sums, square, split)

    for offset, block in zip(near_first(swap_offsets(me_ref[0])), (b0, b1, b2, b3)):
        number = SLOTS * number_of(offset)
        for k in range(SLOTS):
            leaf, a = plan_ref[MIG + number + k], plan_ref[FROM + number + k]
            at = pl.ds(jnp.maximum(leaf, 0), 1)
            held = jnp.full((1, LANES), jnp.where(leaf >= 0, 1, 0), I32) > 0
            live = jnp.full((1, LANES), jnp.where(a >= 0, 1, 0), I32) > 0
            total, center = sums[jnp.maximum(a, 0)], centers[jnp.maximum(a, 0)]
            for c in range(3):
                x, v = points[c, at, :], velocities_ref[c, at, :]
                v = jnp.where(live, kicked(x, v, total, center, c), v)
                block[c, k : k + 1, :] = jnp.where(held, x + 0.25 * v, 0.0)
                block[3 + c, k : k + 1, :] = jnp.where(held, v, 0.0)
            block[6, k : k + 1, :] = jnp.where(held, points[3, at, :], 0.0)


def staying_kernel(plan_ref, points, velocities_ref, sums_in, targets, centers, sources, blocks,
                   new_positions, new_velocities, sums, square, split):
    sums[...] = sums_in[...]
    new_velocities[...] = velocities_ref[...]
    new_positions[...] = points[:3] + 0.25 * velocities_ref[...]
    run_list(plan_ref, STAYING, plan_ref[SIZES + 1], targets, centers, sources, blocks, sums, square, split)

    @pl.loop(0, plan_ref[LIVE])
    def _(a):
        at = pl.ds(plan_ref[ACTIVE + a], 1)
        total, center = sums[a], centers[a]
        for c in range(3):
            x = points[c, at, :]
            v = kicked(x, velocities_ref[c, at, :], total, center, c)
            new_velocities[c, at, :] = v
            new_positions[c, at, :] = x + 0.25 * v


def arrival_kernel(me_ref, c0, c1, c2, c3, out):
    for offset, came in zip(near_first(swap_offsets(me_ref[0])), (c0, c1, c2, c3)):
        out[:, pl.ds(SLOTS * number_of(-offset), SLOTS), :] = came[...]


def shape(*dims, dtype=F32):
    return jax.ShapeDtypeStruct(dims, dtype)


def per_device(positions, velocities, masses, active_leaves, active_count, partner_owner, partner_leaf, mig_leaf):
    leaves = positions.shape[1]
    domains = lax.axis_size("dom")
    me = lax.axis_index("dom").astype(I32)
    dma = pltpu.SemaphoreType.DMA
    *requests, place = pl.pallas_call(
        functools.partial(request_kernel, domains, leaves),
        out_shape=[shape(1, LANES, dtype=I32)] * SIDES + [shape(ACT, PARTNERS, dtype=I32)],
        in_specs=[SMEM, VMEM],
        out_specs=[VMEM] * (SIDES + 1),
        compiler_params=params(4),
        cost_estimate=pl.CostEstimate(flops=10_000_000, bytes_accessed=10_000, transcendentals=0),
        name="requests",
    )(me.reshape(1), partner_owner * OWNER + partner_leaf)
    asked = [swapped(r, p) for r, p in zip(requests, PARTNERS_OF)]
    stage = [pltpu.VMEM((8 * ROWS, LANES), F32)]
    chunks = [pltpu.VMEM((CHUNK, LANES, LANES), F32), pltpu.VMEM((CHUNK, 2 * LANES, LANES), BF16)]
    slot_sums, all_own = shape(ACT, 8, LANES), ACT * PARTNERS
    held = [pltpu.VMEM((48, LANES), F32)]
    points, targets, centers = pl.pallas_call(
        stage_kernel,
        out_shape=[shape(4, leaves, LANES), shape(ACT, ROWS, LANES, dtype=BF16), slot_sums],
        in_specs=[SMEM, VMEM, VMEM, ANY],
        out_specs=[VMEM] * 3,
        scratch_shapes=held + stage,
        compiler_params=params(8),
        cost_estimate=pl.CostEstimate(flops=10_000_000, bytes_accessed=10_000, transcendentals=0),
        name="stage",
    )(active_leaves, positions, masses, place)
    *replies, token = pl.pallas_call(
        reply_kernel,
        out_shape=[shape(4 * IMPORT, LANES)] * SIDES + [shape(1, LANES)],
        in_specs=[SMEM] * SIDES + [VMEM],
        out_specs=[VMEM] * (SIDES + 1),
        compiler_params=params(4),
        name="replies",
    )(*asked, points)
    plan = pl.pallas_call(
        plan_kernel,
        out_shape=shape(PLAN, dtype=I32),
        in_specs=[VMEM] + [SMEM] * 3 + [ANY],
        out_specs=SMEM,
        scratch_shapes=[pltpu.VMEM((ACT, PARTNERS), I32), pltpu.SMEM((ACT, PARTNERS), I32), dma],
        compiler_params=params(4),
        cost_estimate=pl.CostEstimate(flops=10_000_000, bytes_accessed=10_000, transcendentals=0),
        name="plan",
    )(place, active_count, active_leaves, mig_leaf, token)
    received = [swapped(r, p) for r, p in zip(replies, PARTNERS_OF)]
    sums = pl.pallas_call(
        local_kernel,
        out_shape=slot_sums,
        in_specs=[SMEM] + [VMEM] * 3,
        out_specs=VMEM,
        scratch_shapes=held
        + stage
        + [pltpu.VMEM((all_own, LANES, ROWS), BF16), pltpu.VMEM((8 * all_own, LANES), F32)]
        + chunks,
        compiler_params=params(24),
        cost_estimate=pl.CostEstimate(flops=10_000_000, bytes_accessed=10_000, transcendentals=0),
        name="local_pairs",
    )(plan, points, targets, centers)
    sums, sources, tables, *blocks = pl.pallas_call(
        leaving_kernel,
        out_shape=[slot_sums, shape(IMPORTS, LANES, ROWS, dtype=BF16), shape(8 * IMPORTS, LANES)]
        + [shape(7, SLOTS, LANES)] * SIDES,
        in_specs=[SMEM] * 2 + [VMEM] * (5 + SIDES),
        out_specs=[VMEM] * (3 + SIDES),
        scratch_shapes=stage + chunks,
        compiler_params=params(16),
        name="leaving",
    )(me.reshape(1), plan, points, velocities, sums, targets, centers, *received)
    came = [swapped(b, p) for b, p in zip(blocks, near_first(PARTNERS_OF))]
    new_positions, new_velocities = pl.pallas_call(
        staying_kernel,
        out_shape=[shape(3, leaves, LANES)] * 2,
        in_specs=[SMEM] + [VMEM] * 7,
        out_specs=[VMEM] * 2,
        scratch_shapes=[pltpu.VMEM((ACT, 8, LANES), F32)] + chunks,
        compiler_params=params(16),
        cost_estimate=pl.CostEstimate(flops=100_000_000, bytes_accessed=10_000, transcendentals=0),
        name="staying",
    )(plan, points, velocities, sums, targets, centers, sources, tables)
    arrived = pl.pallas_call(
        arrival_kernel,
        out_shape=shape(7, SIDES * SLOTS, LANES),
        in_specs=[SMEM] + [VMEM] * SIDES,
        out_specs=VMEM,
        compiler_params=params(4),
        name="arrivals",
    )(me.reshape(1), *came)
    return new_positions, new_velocities, arrived


def solution(mesh):
    return jax.shard_map(
        per_device,
        mesh=mesh,
        in_specs=(
            P(None, "dom", None),
            P(None, "dom", None),
            P("dom", None),
            P("dom"),
            P("dom"),
            P("dom", None),
            P("dom", None),
            P("dom"),
        ),
        out_specs=(P(None, "dom", None), P(None, "dom", None), P(None, "dom", None)),
        check_vma=False,
    )
```

```python
import functools
import math

import jax
import jax.numpy as jnp
from jax import lax
from jax.experimental import pallas as pl
from jax.experimental.pallas import tpu as pltpu
from jax.sharding import PartitionSpec as P

REACH = 2
SLOTS = 4
IMPORT = 8
ACT = 16
PARTNERS = 16
LANES = 128
SIDES = 2 * REACH
IMPORTS = SIDES * IMPORT
BIG = 1 << 20
OWNER_BIT = 10
OWNER = 1 << OWNER_BIT

soften = 0.02
EPS = 4.0 * soften * soften
NEG_LOG2E = -math.log2(math.e)
TWO_OVER_ROOT_PI = 2.0 / math.sqrt(math.pi)

F32, BF16, I32 = jnp.float32, jnp.bfloat16, jnp.int32

CHUNK = 8
AHEAD = 2 * CHUNK
COARSE, ROWS = 16, 48
LEAVING, STAYING, LOCAL, SIZES, FROM, LIVE, ACTIVE, MIG, PLAN = 0, 304, 608, 912, 920, 936, 937, 953, 969
GIVEN = PLAN - LIVE
SLOT_BIT, PLACE_BIT = 16, 5

VMEM = pl.BlockSpec(memory_space=pltpu.VMEM)
SMEM = pl.BlockSpec(memory_space=pltpu.SMEM)
ANY = pl.BlockSpec(memory_space=pl.ANY)


def params(mib):
    return pltpu.CompilerParams(vmem_limit_bytes=mib << 20)


def swapped(shard, partner):
    return lax.ppermute(shard, "dom", [(i, partner(i) % lax.axis_size("dom")) for i in range(lax.axis_size("dom"))])


PARTNERS_OF = (
    lambda d: d + 2 if d & 2 else d - 2,
    lambda d: d + 1 if d & 1 else d - 1,
    lambda d: d ^ 2,
    lambda d: d ^ 1,
)


def swap_offsets(me):
    one, two = 1 - 2 * (me & 1), 2 - 2 * (me & 2)
    return -two, -one, two, one


def near_first(swaps):
    return [*swaps[2:], *swaps[:2]]


def number_of(offset):
    return offset + jnp.where(offset < 0, REACH, REACH - 1)


def request_kernel(domains, leaves, me_ref, entry_ref, *outs):
    requests, place_ref = outs[:SIDES], outs[SIDES]
    entry = entry_ref[...]
    leaf = entry & (OWNER - 1)
    relative = lax.shift_right_logical(entry, OWNER_BIT) - me_ref[0] + REACH
    relative = jnp.where(relative < 0, relative + domains, relative)
    relative = jnp.where(relative >= domains, relative - domains, relative)
    lane = lax.broadcasted_iota(I32, (1, LANES), 1)
    place = IMPORTS + leaf

    def over_all(reduce, v):
        return reduce(reduce(v, axis=0, keepdims=True), axis=1, keepdims=True)

    for side, offset in enumerate(swap_offsets(me_ref[0])):
        mine = relative == offset + REACH
        low, high = jnp.where(mine, leaf, BIG), jnp.where(mine, leaf, -1)
        rank = jnp.zeros_like(leaf)
        row = jnp.zeros((1, LANES), I32)
        for k in range(IMPORT // 2):
            last = IMPORT - 1 - k
            least, most = over_all(jnp.min, low), over_all(jnp.max, high)
            row = jnp.where(lane == k, jnp.broadcast_to(least, row.shape), row)
            row = jnp.where(lane == last, jnp.broadcast_to(most, row.shape), row)
            rank = jnp.where(low == least, k, jnp.where(high == most, last, rank))
            low = jnp.where(low == least, BIG, low)
            high = jnp.where(high == most, -1, high)
        requests[side][...] = jnp.clip(row, 0, leaves - 1)
        place = jnp.where(mine, side * IMPORT + rank, place)
    place_ref[...] = place


def make_plan(packed_ref, given_ref, plan_ref):
    for i in range(GIVEN):
        plan_ref[LIVE + i] = given_ref[i]
    live = given_ref[0]

    def one_slot(a, carried):
        leaving_end, staying_end, local_end, origins = carried
        leaf = given_ref[ACTIVE - LIVE + a]
        hits = jnp.int32(0)
        found = []
        for n in range(SIDES * SLOTS):
            hit = given_ref[MIG - LIVE + n] == leaf
            found.append(jnp.where(hit, a, origins[n]))
            hits = hits + jnp.where(hit, 1, 0)
        end = jnp.where(hits > 0, leaving_end, staying_end)
        for k in range(PARTNERS):
            packed = packed_ref[a, k]
            word = (a << SLOT_BIT) + packed
            plan_ref[end] = word
            plan_ref[local_end] = word
            counts = jnp.where((packed & 31) > 0, 1, 0)
            remote = jnp.where(packed < (IMPORTS << PLACE_BIT), counts, 0)
            end, local_end = end + remote, local_end + counts - remote
        leaving_end, staying_end = jnp.where(hits > 0, end, leaving_end), jnp.where(hits > 0, staying_end, end)
        return leaving_end, staying_end, local_end, tuple(found)

    ends = [jnp.int32(base + AHEAD) for base in (LEAVING, STAYING, LOCAL)]
    nowhere = tuple(jnp.int32(-1) for _ in range(SIDES * SLOTS))
    *ends, origins = lax.fori_loop(0, live, one_slot, (*ends, nowhere))
    for n, a in enumerate(origins):
        plan_ref[FROM + n] = a
    for i, (base, end) in enumerate(zip((LEAVING, STAYING, LOCAL), ends)):
        for k in range(AHEAD):
            plan_ref[base + k] = 0
        for k in range(3 * CHUNK):
            plan_ref[end + k] = 0
        plan_ref[SIZES + i] = end - (base + AHEAD)


def reply_kernel(r0, r1, r2, r3, points, o0, o1, o2, o3, token):
    token[...] = jnp.zeros_like(token)
    for request, out in ((r0, o0), (r1, o1), (r2, o2), (r3, o3)):
        for k in range(IMPORT):
            at = pl.ds(request[0, k], 1)
            for c in range(3):
                out[8 * c + k : 8 * c + k + 1, :] = 2.0 * points[c, at, :]
            out[24 + k : 25 + k, :] = points[3, at, :]


def pieces(v):
    a = v.astype(BF16).astype(F32)
    b = (v - a).astype(BF16).astype(F32)
    return a, b, v - a - b


def split_rows(xs):
    h = [jnp.floor(x * 128.0 + 0.5) * (1.0 / 128.0) for x in xs]
    l = [x - y for x, y in zip(xs, h)]
    l1 = [v.astype(BF16).astype(F32) for v in l]
    l2 = [v - w for v, w in zip(l, l1)]
    coarse = h[0] * h[0] + h[1] * h[1] + h[2] * h[2]
    fine = sum(b * (2.0 * a + b) for a, b in zip(h, l))
    return h, l1, l2, coarse, fine


def times_minus_two(rows):
    return [-2.0 * r for r in rows]


def source_rows(xs):
    h, l1, l2, coarse, fine = split_rows(xs)
    one, none = jnp.ones_like(coarse), [None]
    first = times_minus_two(h) + [*pieces(coarse), one, one, one] + none * 7
    return first + [*h, *h, *l1, *l2, *l1, *l1, *l2, *l2, *pieces(fine), one, one, one] + none * 2


def target_rows(xs):
    h, l1, l2, coarse, fine = split_rows(xs)
    one, none = jnp.ones_like(coarse), [None]
    first = h + [one, one, one, *pieces(coarse)] + none * 7
    n1, n2, nh = times_minus_two(l1), times_minus_two(l2), times_minus_two(h)
    return first + [*n1, *n2, *nh, *nh, *n1, *n2, *n1, *n2, one, one, one, *pieces(fine + EPS)] + none * 2


def by_leaf(stage, rows, start=0):
    for r, row in enumerate(rows):
        stage[pl.ds(start + r, 8, stride=len(rows)), :] = jnp.zeros((8, LANES), F32) if row is None else row


def set_sources(first, xs, m, stage, sources, blocks):
    by_leaf(stage, source_rows(xs))
    pad = jnp.zeros((LANES - ROWS, LANES), F32)
    for k in range(8):
        wide = jnp.concatenate([stage[ROWS * k : ROWS * (k + 1), :], pad], axis=0)
        sources[first + k] = jnp.transpose(wide)[:, :ROWS].astype(BF16)
    rows = [*xs, jnp.ones_like(m), m] + [None] * 3
    by_leaf(blocks, rows, start=8 * first)


def run_list(plan_ref, base, n, targets, centers, sources, blocks, sums, square, split, by_position=False):
    square[...] = jnp.ones_like(square)
    split[...] = jnp.zeros_like(split)

    def fields(word, position):
        place = jnp.clip(position, 0, n - 1) if by_position else lax.shift_right_logical(word, PLACE_BIT) & 1023
        return lax.shift_right_logical(word, SLOT_BIT), place

    @pl.loop(0, lax.shift_right_logical(n + CHUNK - 1, 3) + 2)
    def _(q):
        start = base + q * CHUNK
        for t in range(CHUNK):
            word = plan_ref[start + t]
            slot, place = fields(word, q * CHUNK + t - AHEAD)
            block = blocks[pl.ds(pl.multiple_of(8 * place, 8), 8), :]
            mass = block[4:5] * (word & 31).astype(F32)
            a, b, c = pieces((block - centers[slot]) * mass)
            weights = jnp.concatenate([a, b, c, jnp.zeros_like(c)], axis=0).astype(BF16)
            out = jnp.dot(jnp.concatenate([weights, weights], axis=1), split[t], preferred_element_type=F32)
            sums[slot] += out[0:8] + out[8:16] + out[16:24]
        for t in range(CHUNK):
            sq = square[t]
            inverse = lax.rsqrt(sq)
            gauss = TWO_OVER_ROOT_PI * jnp.exp2(sq * NEG_LOG2E)
            law = ((1.0 - lax.erf(sq * inverse)) * inverse + gauss) * (inverse * inverse)
            high = law.astype(BF16)
            split[t, :LANES] = high
            split[t, LANES:] = (law - high.astype(F32)).astype(BF16)
        for t in range(CHUNK):
            slot, place = fields(plan_ref[start + AHEAD + t], q * CHUNK + t)
            square[t] = jnp.dot(
                sources[place, :, :COARSE], targets[slot, :COARSE], preferred_element_type=F32
            ) + jnp.dot(sources[place, :, COARSE:], targets[slot, COARSE:], preferred_element_type=F32)


def stage_kernel(count_ref, active_ref, mig_ref, positions_ref, masses_ref, place_ref,
                 points, targets, centers, packed_ref, given_ref, held, stage):
    given_ref[0] = count_ref[0]
    for a in range(ACT):
        given_ref[ACTIVE - LIVE + a] = active_ref[a]
    for n in range(SIDES * SLOTS):
        given_ref[MIG - LIVE + n] = mig_ref[n]
    place = place_ref[...]
    column = lax.broadcasted_iota(I32, place.shape, 1)
    times = jnp.zeros_like(place)
    earlier = jnp.zeros_like(place)
    for k in range(PARTNERS):
        same = (place == place[:, k : k + 1]).astype(I32)
        times = times + same
        earlier = jnp.where(column > k, earlier + same, earlier)
    packed_ref[...] = (place << PLACE_BIT) + jnp.where(earlier > 0, 0, times)
    points[:3] = positions_ref[...]
    points[3] = masses_ref[...]
    for a in range(ACT):
        at = pl.ds(active_ref[a], 1)
        for c in range(3):
            held[16 * c + a : 16 * c + a + 1, :] = 2.0 * positions_ref[c, at, :]
    for g in range(ACT // 8):
        xs = [held[16 * c + 8 * g : 16 * c + 8 * g + 8, :] for c in range(3)]
        by_leaf(stage, target_rows(xs))
        for k in range(8):
            targets[8 * g + k] = stage[ROWS * k : ROWS * (k + 1), :].astype(BF16)
        means = [jnp.broadcast_to(jnp.mean(x, axis=1, keepdims=True), x.shape) for x in xs]
        by_leaf(stage, means + [None] * 5)
        for k in range(8):
            centers[8 * g + k] = stage[8 * k : 8 * k + 8, :]


def local_kernel(packed_ref, given_ref, points, targets, centers, _,
                 plan_ref, sums, held, stage, sources, blocks, square, split):
    make_plan(packed_ref, given_ref, plan_ref)
    sums[...] = jnp.zeros_like(sums)
    n = plan_ref[SIZES + 2]

    @pl.when(n > 0)
    def _():
        @pl.loop(0, lax.shift_right_logical(n + 7, 3))
        def _(g):
            for k in range(8):
                word = plan_ref[LOCAL + AHEAD + 8 * g + k]
                leaf = (lax.shift_right_logical(word, PLACE_BIT) & 1023) - IMPORTS
                at = pl.ds(jnp.maximum(leaf, 0), 1)
                for c in range(3):
                    held[8 * c + k : 8 * c + k + 1, :] = 2.0 * points[c, at, :]
                held[24 + k : 25 + k, :] = points[3, at, :]
            xs = [held[8 * c : 8 * c + 8, :] for c in range(3)]
            set_sources(pl.multiple_of(8 * g, 8), xs, held[24:32, :], stage, sources, blocks)

        run_list(plan_ref, LOCAL, n, targets, centers, sources, blocks, sums, square, split, by_position=True)


def kicked(x, v, total, center, c):
    return v + (total[c : c + 1] - (2.0 * x - center[c : c + 1]) * total[3:4])


def leaving_kernel(me_ref, plan_ref, points, velocities_ref, sums_in, targets, centers, r0, r1, r2, r3,
                   sums, sources, blocks, b0, b1, b2, b3, stage, square, split):
    for side, received in enumerate((r0, r1, r2, r3)):
        xs = [received[8 * c : 8 * c + 8, :] for c in range(3)]
        set_sources(8 * side, xs, received[24:32, :], stage, sources, blocks)
    sums[...] = sums_in[...]
    n_leaving = plan_ref[SIZES]

    @pl.when(n_leaving > 0)
    def _():
        run_list(plan_ref, LEAVING, n_leaving, targets, centers, sources, blocks, sums, square, split)

    for offset, block in zip(near_first(swap_offsets(me_ref[0])), (b0, b1, b2, b3)):
        number = SLOTS * number_of(offset)
        for k in range(SLOTS):
            leaf, a = plan_ref[MIG + number + k], plan_ref[FROM + number + k]
            at = pl.ds(jnp.maximum(leaf, 0), 1)
            held = jnp.full((1, LANES), jnp.where(leaf >= 0, 1, 0), I32) > 0
            live = jnp.full((1, LANES), jnp.where(a >= 0, 1, 0), I32) > 0
            total, center = sums[jnp.maximum(a, 0)], centers[jnp.maximum(a, 0)]
            for c in range(3):
                x, v = points[c, at, :], velocities_ref[c, at, :]
                v = jnp.where(live, kicked(x, v, total, center, c), v)
                block[c, k : k + 1, :] = jnp.where(held, x + 0.25 * v, 0.0)
                block[3 + c, k : k + 1, :] = jnp.where(held, v, 0.0)
            block[6, k : k + 1, :] = jnp.where(held, points[3, at, :], 0.0)


def staying_kernel(plan_ref, points, velocities_ref, sums_in, targets, centers, sources, blocks,
                   new_positions, new_velocities, sums, square, split):
    sums[...] = sums_in[...]
    new_velocities[...] = velocities_ref[...]
    new_positions[...] = points[:3] + 0.25 * velocities_ref[...]
    run_list(plan_ref, STAYING, plan_ref[SIZES + 1], targets, centers, sources, blocks, sums, square, split)

    @pl.loop(0, plan_ref[LIVE])
    def _(a):
        at = pl.ds(plan_ref[ACTIVE + a], 1)
        total, center = sums[a], centers[a]
        for c in range(3):
            x = points[c, at, :]
            v = kicked(x, velocities_ref[c, at, :], total, center, c)
            new_velocities[c, at, :] = v
            new_positions[c, at, :] = x + 0.25 * v


def arrival_kernel(me_ref, c0, c1, c2, c3, out):
    for offset, came in zip(near_first(swap_offsets(me_ref[0])), (c0, c1, c2, c3)):
        out[:, pl.ds(SLOTS * number_of(-offset), SLOTS), :] = came[...]


def shape(*dims, dtype=F32):
    return jax.ShapeDtypeStruct(dims, dtype)


def per_device(positions, velocities, masses, active_leaves, active_count, partner_owner, partner_leaf, mig_leaf):
    leaves = positions.shape[1]
    domains = lax.axis_size("dom")
    me = lax.axis_index("dom").astype(I32)
    *requests, place = pl.pallas_call(
        functools.partial(request_kernel, domains, leaves),
        out_shape=[shape(1, LANES, dtype=I32)] * SIDES + [shape(ACT, PARTNERS, dtype=I32)],
        in_specs=[SMEM, VMEM],
        out_specs=[VMEM] * (SIDES + 1),
        compiler_params=params(4),
        cost_estimate=pl.CostEstimate(flops=3_000_000_000, bytes_accessed=10_000, transcendentals=0),
        name="requests",
    )(me.reshape(1), partner_owner * OWNER + partner_leaf)
    asked = [swapped(r, p) for r, p in zip(requests, PARTNERS_OF)]
    stage = [pltpu.VMEM((8 * ROWS, LANES), F32)]
    chunks = [pltpu.VMEM((CHUNK, LANES, LANES), F32), pltpu.VMEM((CHUNK, 2 * LANES, LANES), BF16)]
    slot_sums, all_own = shape(ACT, 8, LANES), ACT * PARTNERS
    held = [pltpu.VMEM((48, LANES), F32)]
    points, targets, centers, packed, given = pl.pallas_call(
        stage_kernel,
        out_shape=[
            shape(4, leaves, LANES),
            shape(ACT, ROWS, LANES, dtype=BF16),
            slot_sums,
            shape(ACT, PARTNERS, dtype=I32),
            shape(GIVEN, dtype=I32),
        ],
        in_specs=[SMEM] * 3 + [VMEM] * 3,
        out_specs=[VMEM] * 4 + [SMEM],
        scratch_shapes=held + stage,
        compiler_params=params(8),
        cost_estimate=pl.CostEstimate(flops=3_000_000_000, bytes_accessed=10_000, transcendentals=0),
        name="stage",
    )(active_count, active_leaves, mig_leaf, positions, masses, place)
    *replies, token = pl.pallas_call(
        reply_kernel,
        out_shape=[shape(4 * IMPORT, LANES)] * SIDES + [shape(1, LANES)],
        in_specs=[SMEM] * SIDES + [VMEM],
        out_specs=[VMEM] * (SIDES + 1),
        compiler_params=params(4),
        name="replies",
    )(*asked, points)
    received = [swapped(r, p) for r, p in zip(replies, PARTNERS_OF)]
    plan, sums = pl.pallas_call(
        local_kernel,
        out_shape=[shape(PLAN, dtype=I32), slot_sums],
        in_specs=[SMEM] * 2 + [VMEM] * 3 + [ANY],
        out_specs=[SMEM, VMEM],
        scratch_shapes=held
        + stage
        + [pltpu.VMEM((all_own, LANES, ROWS), BF16), pltpu.VMEM((8 * all_own, LANES), F32)]
        + chunks,
        compiler_params=params(24),
        cost_estimate=pl.CostEstimate(flops=4_000_000_000, bytes_accessed=10_000, transcendentals=0),
        name="local_pairs",
    )(packed, given, points, targets, centers, token)
    sums, sources, tables, *blocks = pl.pallas_call(
        leaving_kernel,
        out_shape=[slot_sums, shape(IMPORTS, LANES, ROWS, dtype=BF16), shape(8 * IMPORTS, LANES)]
        + [shape(7, SLOTS, LANES)] * SIDES,
        in_specs=[SMEM] * 2 + [VMEM] * (5 + SIDES),
        out_specs=[VMEM] * (3 + SIDES),
        scratch_shapes=stage + chunks,
        compiler_params=params(16),
        name="leaving",
    )(me.reshape(1), plan, points, velocities, sums, targets, centers, *received)
    came = [swapped(b, p) for b, p in zip(blocks, near_first(PARTNERS_OF))]
    new_positions, new_velocities = pl.pallas_call(
        staying_kernel,
        out_shape=[shape(3, leaves, LANES)] * 2,
        in_specs=[SMEM] + [VMEM] * 7,
        out_specs=[VMEM] * 2,
        scratch_shapes=[pltpu.VMEM((ACT, 8, LANES), F32)] + chunks,
        compiler_params=params(16),
        cost_estimate=pl.CostEstimate(flops=7_000_000_000, bytes_accessed=10_000, transcendentals=0),
        name="staying",
    )(plan, points, velocities, sums, targets, centers, sources, tables)
    arrived = pl.pallas_call(
        arrival_kernel,
        out_shape=shape(7, SIDES * SLOTS, LANES),
        in_specs=[SMEM] + [VMEM] * SIDES,
        out_specs=VMEM,
        compiler_params=params(4),
        name="arrivals",
    )(me.reshape(1), *came)
    return new_positions, new_velocities, arrived


def solution(mesh):
    return jax.shard_map(
        per_device,
        mesh=mesh,
        in_specs=(
            P(None, "dom", None),
            P(None, "dom", None),
            P("dom", None),
            P("dom"),
            P("dom"),
            P("dom", None),
            P("dom", None),
            P("dom"),
        ),
        out_specs=(P(None, "dom", None), P(None, "dom", None), P(None, "dom", None)),
        check_vma=False,
    )
```

```python
import functools
import math

import jax
import jax.numpy as jnp
from jax import lax
from jax.experimental import pallas as pl
from jax.experimental.pallas import tpu as pltpu
from jax.sharding import PartitionSpec as P

REACH = 2
SLOTS = 4
IMPORT = 8
ACT = 16
PARTNERS = 16
LANES = 128
SIDES = 2 * REACH
IMPORTS = SIDES * IMPORT
BIG = 1 << 20
OWNER_BIT = 10
OWNER = 1 << OWNER_BIT

soften = 0.02
EPS = 4.0 * soften * soften
NEG_LOG2E = -math.log2(math.e)
TWO_OVER_ROOT_PI = 2.0 / math.sqrt(math.pi)

F32, BF16, I32 = jnp.float32, jnp.bfloat16, jnp.int32

CHUNK = 8
COARSE, ROWS = 16, 48
LEAVING, STAYING, LOCAL, SIZES, FROM, LIVE, ACTIVE, MIG, PLAN = 0, 304, 608, 912, 920, 936, 937, 953, 969
GIVEN = PLAN - LIVE
SLOT_BIT, PLACE_BIT = 16, 5

VMEM = pl.BlockSpec(memory_space=pltpu.VMEM)
SMEM = pl.BlockSpec(memory_space=pltpu.SMEM)
ANY = pl.BlockSpec(memory_space=pl.ANY)


def params(mib):
    return pltpu.CompilerParams(vmem_limit_bytes=mib << 20)


def swapped(shard, partner):
    return lax.ppermute(shard, "dom", [(i, partner(i) % lax.axis_size("dom")) for i in range(lax.axis_size("dom"))])


PARTNERS_OF = (
    lambda d: d + 2 if d & 2 else d - 2,
    lambda d: d + 1 if d & 1 else d - 1,
    lambda d: d ^ 2,
    lambda d: d ^ 1,
)


def swap_offsets(me):
    one, two = 1 - 2 * (me & 1), 2 - 2 * (me & 2)
    return -two, -one, two, one


def near_first(swaps):
    return [*swaps[2:], *swaps[:2]]


def number_of(offset):
    return offset + jnp.where(offset < 0, REACH, REACH - 1)


def request_kernel(domains, leaves, me_ref, entry_ref, *outs):
    requests, place_ref = outs[:SIDES], outs[SIDES]
    entry = entry_ref[...]
    leaf = entry & (OWNER - 1)
    relative = lax.shift_right_logical(entry, OWNER_BIT) - me_ref[0] + REACH
    relative = jnp.where(relative < 0, relative + domains, relative)
    relative = jnp.where(relative >= domains, relative - domains, relative)
    lane = lax.broadcasted_iota(I32, (1, LANES), 1)
    place = IMPORTS + leaf

    def over_all(reduce, v):
        return reduce(reduce(v, axis=0, keepdims=True), axis=1, keepdims=True)

    for side, offset in enumerate(swap_offsets(me_ref[0])):
        mine = relative == offset + REACH
        low, high = jnp.where(mine, leaf, BIG), jnp.where(mine, leaf, -1)
        rank = jnp.zeros_like(leaf)
        row = jnp.zeros((1, LANES), I32)
        for k in range(IMPORT // 2):
            last = IMPORT - 1 - k
            least, most = over_all(jnp.min, low), over_all(jnp.max, high)
            row = jnp.where(lane == k, jnp.broadcast_to(least, row.shape), row)
            row = jnp.where(lane == last, jnp.broadcast_to(most, row.shape), row)
            rank = jnp.where(low == least, k, jnp.where(high == most, last, rank))
            low = jnp.where(low == least, BIG, low)
            high = jnp.where(high == most, -1, high)
        requests[side][...] = jnp.clip(row, 0, leaves - 1)
        place = jnp.where(mine, side * IMPORT + rank, place)
    place_ref[...] = place


def make_plan(packed_ref, given_ref, plan_ref):
    for i in range(GIVEN):
        plan_ref[LIVE + i] = given_ref[i]
    live = given_ref[0]

    def one_slot(a, carried):
        leaving_end, staying_end, local_end, origins = carried
        leaf = given_ref[ACTIVE - LIVE + a]
        hits = jnp.int32(0)
        found = []
        for n in range(SIDES * SLOTS):
            hit = given_ref[MIG - LIVE + n] == leaf
            found.append(jnp.where(hit, a, origins[n]))
            hits = hits + jnp.where(hit, 1, 0)
        end = jnp.where(hits > 0, leaving_end, staying_end)
        for k in range(PARTNERS):
            packed = packed_ref[a, k]
            word = (a << SLOT_BIT) + packed
            plan_ref[end] = word
            plan_ref[local_end] = word
            counts = jnp.where((packed & 31) > 0, 1, 0)
            remote = jnp.where(packed < (IMPORTS << PLACE_BIT), counts, 0)
            end, local_end = end + remote, local_end + counts - remote
        leaving_end, staying_end = jnp.where(hits > 0, end, leaving_end), jnp.where(hits > 0, staying_end, end)
        return leaving_end, staying_end, local_end, tuple(found)

    ends = [jnp.int32(base) for base in (LEAVING, STAYING, LOCAL)]
    nowhere = tuple(jnp.int32(-1) for _ in range(SIDES * SLOTS))
    *ends, origins = lax.fori_loop(0, live, one_slot, (*ends, nowhere))
    for n, a in enumerate(origins):
        plan_ref[FROM + n] = a
    for i, (base, end) in enumerate(zip((LEAVING, STAYING, LOCAL), ends)):
        for k in range(3 * CHUNK):
            plan_ref[end + k] = 0
        plan_ref[SIZES + i] = end - base


def reply_kernel(r0, r1, r2, r3, points, o0, o1, o2, o3, token):
    token[...] = jnp.zeros_like(token)
    for request, out in ((r0, o0), (r1, o1), (r2, o2), (r3, o3)):
        for k in range(IMPORT):
            at = pl.ds(request[0, k], 1)
            for c in range(3):
                out[8 * c + k : 8 * c + k + 1, :] = 2.0 * points[c, at, :]
            out[24 + k : 25 + k, :] = points[3, at, :]


def pieces(v):
    a = v.astype(BF16).astype(F32)
    b = (v - a).astype(BF16).astype(F32)
    return a, b, v - a - b


def split_rows(xs):
    h = [jnp.floor(x * 128.0 + 0.5) * (1.0 / 128.0) for x in xs]
    l = [x - y for x, y in zip(xs, h)]
    l1 = [v.astype(BF16).astype(F32) for v in l]
    l2 = [v - w for v, w in zip(l, l1)]
    coarse = h[0] * h[0] + h[1] * h[1] + h[2] * h[2]
    fine = sum(b * (2.0 * a + b) for a, b in zip(h, l))
    return h, l1, l2, coarse, fine


def times_minus_two(rows):
    return [-2.0 * r for r in rows]


def source_rows(xs):
    h, l1, l2, coarse, fine = split_rows(xs)
    one, none = jnp.ones_like(coarse), [None]
    first = times_minus_two(h) + [*pieces(coarse), one, one, one] + none * 7
    return first + [*h, *h, *l1, *l2, *l1, *l1, *l2, *l2, *pieces(fine), one, one, one] + none * 2


def target_rows(xs):
    h, l1, l2, coarse, fine = split_rows(xs)
    one, none = jnp.ones_like(coarse), [None]
    first = h + [one, one, one, *pieces(coarse)] + none * 7
    n1, n2, nh = times_minus_two(l1), times_minus_two(l2), times_minus_two(h)
    return first + [*n1, *n2, *nh, *nh, *n1, *n2, *n1, *n2, one, one, one, *pieces(fine + EPS)] + none * 2


def by_leaf(stage, rows, start=0):
    for r, row in enumerate(rows):
        stage[pl.ds(start + r, 8, stride=len(rows)), :] = jnp.zeros((8, LANES), F32) if row is None else row


def set_sources(first, xs, m, stage, sources, blocks):
    by_leaf(stage, source_rows(xs))
    pad = jnp.zeros((LANES - ROWS, LANES), F32)
    for k in range(8):
        wide = jnp.concatenate([stage[ROWS * k : ROWS * (k + 1), :], pad], axis=0)
        sources[first + k] = jnp.transpose(wide)[:, :ROWS].astype(BF16)
    rows = [*xs, jnp.ones_like(m), m] + [None] * 3
    by_leaf(blocks, rows, start=8 * first)


def run_list(plan_ref, base, n, targets, centers, sources, blocks, sums, square, split, by_position=False):
    def entry(q, t):
        at = q * CHUNK + t
        word = plan_ref[base + at]
        place = jnp.minimum(at, n - 1) if by_position else lax.shift_right_logical(word, PLACE_BIT) & 1023
        return lax.shift_right_logical(word, SLOT_BIT), place, (word & 31).astype(F32)

    def distances(q):
        for t in range(CHUNK):
            slot, place, _ = entry(q, t)
            square[t] = jnp.dot(
                sources[place, :, :COARSE], targets[slot, :COARSE], preferred_element_type=F32
            ) + jnp.dot(sources[place, :, COARSE:], targets[slot, COARSE:], preferred_element_type=F32)

    def force_law():
        for t in range(CHUNK):
            sq = square[t]
            inverse = lax.rsqrt(sq)
            gauss = TWO_OVER_ROOT_PI * jnp.exp2(sq * NEG_LOG2E)
            law = ((1.0 - lax.erf(sq * inverse)) * inverse + gauss) * (inverse * inverse)
            high = law.astype(BF16)
            split[t, :LANES] = high
            split[t, LANES:] = (law - high.astype(F32)).astype(BF16)

    def add_up(q):
        for t in range(CHUNK):
            slot, place, times = entry(q, t)
            block = blocks[pl.ds(pl.multiple_of(8 * place, 8), 8), :]
            a, b, c = pieces((block - centers[slot]) * (block[4:5] * times))
            weights = jnp.concatenate([a, b, c, jnp.zeros_like(c)], axis=0).astype(BF16)
            out = jnp.dot(jnp.concatenate([weights, weights], axis=1), split[t], preferred_element_type=F32)
            sums[slot] += out[0:8] + out[8:16] + out[16:24]

    chunks = jnp.maximum(lax.shift_right_logical(n + CHUNK - 1, 3), 2)
    distances(0)
    force_law()
    distances(1)

    @pl.loop(2, chunks)
    def _(q):
        add_up(q - 2)
        force_law()
        distances(q)

    add_up(chunks - 2)
    force_law()
    add_up(chunks - 1)


def stage_kernel(given_ref, positions_ref, masses_ref, place_ref, points, targets, centers, packed_ref, held, stage):
    place = place_ref[...]
    column = lax.broadcasted_iota(I32, place.shape, 1)
    times = jnp.zeros_like(place)
    earlier = jnp.zeros_like(place)
    for k in range(PARTNERS):
        same = (place == place[:, k : k + 1]).astype(I32)
        times = times + same
        earlier = jnp.where(column > k, earlier + same, earlier)
    packed_ref[...] = (place << PLACE_BIT) + jnp.where(earlier > 0, 0, times)
    points[:3] = positions_ref[...]
    points[3] = masses_ref[...]
    for a in range(ACT):
        at = pl.ds(given_ref[ACTIVE - LIVE + a], 1)
        for c in range(3):
            held[16 * c + a : 16 * c + a + 1, :] = 2.0 * positions_ref[c, at, :]
    for g in range(ACT // 8):
        xs = [held[16 * c + 8 * g : 16 * c + 8 * g + 8, :] for c in range(3)]
        by_leaf(stage, target_rows(xs))
        for k in range(8):
            targets[8 * g + k] = stage[ROWS * k : ROWS * (k + 1), :].astype(BF16)
        means = [jnp.broadcast_to(jnp.mean(x, axis=1, keepdims=True), x.shape) for x in xs]
        by_leaf(stage, means + [None] * 5)
        for k in range(8):
            centers[8 * g + k] = stage[8 * k : 8 * k + 8, :]


def local_kernel(packed_ref, given_ref, points, targets, centers, _,
                 plan_ref, sums, held, stage, sources, blocks, square, split):
    make_plan(packed_ref, given_ref, plan_ref)
    sums[...] = jnp.zeros_like(sums)
    n = plan_ref[SIZES + 2]

    @pl.when(n > 0)
    def _():
        @pl.loop(0, lax.shift_right_logical(n + 7, 3))
        def _(g):
            for k in range(8):
                word = plan_ref[LOCAL + 8 * g + k]
                leaf = (lax.shift_right_logical(word, PLACE_BIT) & 1023) - IMPORTS
                at = pl.ds(jnp.maximum(leaf, 0), 1)
                for c in range(3):
                    held[8 * c + k : 8 * c + k + 1, :] = 2.0 * points[c, at, :]
                held[24 + k : 25 + k, :] = points[3, at, :]
            xs = [held[8 * c : 8 * c + 8, :] for c in range(3)]
            set_sources(pl.multiple_of(8 * g, 8), xs, held[24:32, :], stage, sources, blocks)

        run_list(plan_ref, LOCAL, n, targets, centers, sources, blocks, sums, square, split, by_position=True)


def kicked(x, v, total, center, c):
    return v + (total[c : c + 1] - (2.0 * x - center[c : c + 1]) * total[3:4])


def leaving_kernel(me_ref, plan_ref, points, velocities_ref, sums_in, targets, centers, r0, r1, r2, r3,
                   sums, sources, blocks, b0, b1, b2, b3, stage, square, split):
    for side, received in enumerate((r0, r1, r2, r3)):
        xs = [received[8 * c : 8 * c + 8, :] for c in range(3)]
        set_sources(8 * side, xs, received[24:32, :], stage, sources, blocks)
    sums[...] = sums_in[...]
    n_leaving = plan_ref[SIZES]

    @pl.when(n_leaving > 0)
    def _():
        run_list(plan_ref, LEAVING, n_leaving, targets, centers, sources, blocks, sums, square, split)

    for offset, block in zip(near_first(swap_offsets(me_ref[0])), (b0, b1, b2, b3)):
        number = SLOTS * number_of(offset)
        for k in range(SLOTS):
            leaf, a = plan_ref[MIG + number + k], plan_ref[FROM + number + k]
            at = pl.ds(jnp.maximum(leaf, 0), 1)
            held = jnp.full((1, LANES), jnp.where(leaf >= 0, 1, 0), I32) > 0
            live = jnp.full((1, LANES), jnp.where(a >= 0, 1, 0), I32) > 0
            total, center = sums[jnp.maximum(a, 0)], centers[jnp.maximum(a, 0)]
            for c in range(3):
                x, v = points[c, at, :], velocities_ref[c, at, :]
                v = jnp.where(live, kicked(x, v, total, center, c), v)
                block[c, k : k + 1, :] = jnp.where(held, x + 0.25 * v, 0.0)
                block[3 + c, k : k + 1, :] = jnp.where(held, v, 0.0)
            block[6, k : k + 1, :] = jnp.where(held, points[3, at, :], 0.0)


def staying_kernel(plan_ref, points, velocities_ref, sums_in, targets, centers, sources, blocks,
                   new_positions, new_velocities, sums, square, split):
    sums[...] = sums_in[...]
    new_velocities[...] = velocities_ref[...]
    new_positions[...] = points[:3] + 0.25 * velocities_ref[...]
    run_list(plan_ref, STAYING, plan_ref[SIZES + 1], targets, centers, sources, blocks, sums, square, split)

    @pl.loop(0, plan_ref[LIVE])
    def _(a):
        at = pl.ds(plan_ref[ACTIVE + a], 1)
        total, center = sums[a], centers[a]
        for c in range(3):
            x = points[c, at, :]
            v = kicked(x, velocities_ref[c, at, :], total, center, c)
            new_velocities[c, at, :] = v
            new_positions[c, at, :] = x + 0.25 * v


def arrival_kernel(me_ref, c0, c1, c2, c3, out):
    for offset, came in zip(near_first(swap_offsets(me_ref[0])), (c0, c1, c2, c3)):
        out[:, pl.ds(SLOTS * number_of(-offset), SLOTS), :] = came[...]


def shape(*dims, dtype=F32):
    return jax.ShapeDtypeStruct(dims, dtype)


def per_device(positions, velocities, masses, active_leaves, active_count, partner_owner, partner_leaf, mig_leaf):
    leaves = positions.shape[1]
    domains = lax.axis_size("dom")
    me = lax.axis_index("dom").astype(I32)
    *requests, place = pl.pallas_call(
        functools.partial(request_kernel, domains, leaves),
        out_shape=[shape(1, LANES, dtype=I32)] * SIDES + [shape(ACT, PARTNERS, dtype=I32)],
        in_specs=[SMEM, VMEM],
        out_specs=[VMEM] * (SIDES + 1),
        compiler_params=params(4),
        cost_estimate=pl.CostEstimate(flops=3_000_000_000, bytes_accessed=10_000, transcendentals=0),
        name="requests",
    )(me.reshape(1), partner_owner * OWNER + partner_leaf)
    asked = [swapped(r, p) for r, p in zip(requests, PARTNERS_OF)]
    stage = [pltpu.VMEM((8 * ROWS, LANES), F32)]
    chunks = [pltpu.VMEM((CHUNK, LANES, LANES), F32), pltpu.VMEM((CHUNK, 2 * LANES, LANES), BF16)]
    slot_sums, all_own = shape(ACT, 8, LANES), ACT * PARTNERS
    held = [pltpu.VMEM((48, LANES), F32)]
    given = jnp.concatenate([active_count, active_leaves, mig_leaf])
    points, targets, centers, packed = pl.pallas_call(
        stage_kernel,
        out_shape=[
            shape(4, leaves, LANES),
            shape(ACT, ROWS, LANES, dtype=BF16),
            slot_sums,
            shape(ACT, PARTNERS, dtype=I32),
        ],
        in_specs=[SMEM] + [VMEM] * 3,
        out_specs=[VMEM] * 4,
        scratch_shapes=held + stage,
        compiler_params=params(8),
        cost_estimate=pl.CostEstimate(flops=3_000_000_000, bytes_accessed=10_000, transcendentals=0),
        name="stage",
    )(given, positions, masses, place)
    *replies, token = pl.pallas_call(
        reply_kernel,
        out_shape=[shape(4 * IMPORT, LANES)] * SIDES + [shape(1, LANES)],
        in_specs=[SMEM] * SIDES + [VMEM],
        out_specs=[VMEM] * (SIDES + 1),
        compiler_params=params(4),
        name="replies",
    )(*asked, points)
    received = [swapped(r, p) for r, p in zip(replies, PARTNERS_OF)]
    plan, sums = pl.pallas_call(
        local_kernel,
        out_shape=[shape(PLAN, dtype=I32), slot_sums],
        in_specs=[SMEM] * 2 + [VMEM] * 3 + [ANY],
        out_specs=[SMEM, VMEM],
        scratch_shapes=held
        + stage
        + [pltpu.VMEM((all_own, LANES, ROWS), BF16), pltpu.VMEM((8 * all_own, LANES), F32)]
        + chunks,
        compiler_params=params(24),
        cost_estimate=pl.CostEstimate(flops=4_000_000_000, bytes_accessed=10_000, transcendentals=0),
        name="local_pairs",
    )(packed, given, points, targets, centers, token)
    sums, sources, tables, *blocks = pl.pallas_call(
        leaving_kernel,
        out_shape=[slot_sums, shape(IMPORTS, LANES, ROWS, dtype=BF16), shape(8 * IMPORTS, LANES)]
        + [shape(7, SLOTS, LANES)] * SIDES,
        in_specs=[SMEM] * 2 + [VMEM] * (5 + SIDES),
        out_specs=[VMEM] * (3 + SIDES),
        scratch_shapes=stage + chunks,
        compiler_params=params(16),
        name="leaving",
    )(me.reshape(1), plan, points, velocities, sums, targets, centers, *received)
    came = [swapped(b, p) for b, p in zip(blocks, near_first(PARTNERS_OF))]
    new_positions, new_velocities = pl.pallas_call(
        staying_kernel,
        out_shape=[shape(3, leaves, LANES)] * 2,
        in_specs=[SMEM] + [VMEM] * 7,
        out_specs=[VMEM] * 2,
        scratch_shapes=[pltpu.VMEM((ACT, 8, LANES), F32)] + chunks,
        compiler_params=params(16),
        cost_estimate=pl.CostEstimate(flops=7_000_000_000, bytes_accessed=10_000, transcendentals=0),
        name="staying",
    )(plan, points, velocities, sums, targets, centers, sources, tables)
    arrived = pl.pallas_call(
        arrival_kernel,
        out_shape=shape(7, SIDES * SLOTS, LANES),
        in_specs=[SMEM] + [VMEM] * SIDES,
        out_specs=VMEM,
        compiler_params=params(4),
        name="arrivals",
    )(me.reshape(1), *came)
    return new_positions, new_velocities, arrived


def solution(mesh):
    return jax.shard_map(
        per_device,
        mesh=mesh,
        in_specs=(
            P(None, "dom", None),
            P(None, "dom", None),
            P("dom", None),
            P("dom"),
            P("dom"),
            P("dom", None),
            P("dom", None),
            P("dom"),
        ),
        out_specs=(P(None, "dom", None), P(None, "dom", None), P(None, "dom", None)),
        check_vma=False,
    )
```

```python
import functools
import math

import jax
import jax.numpy as jnp
from jax import lax
from jax.experimental import pallas as pl
from jax.experimental.pallas import tpu as pltpu
from jax.sharding import PartitionSpec as P

REACH = 2
SLOTS = 4
IMPORT = 8
ACT = 16
PARTNERS = 16
LANES = 128
SIDES = 2 * REACH
IMPORTS = SIDES * IMPORT
BIG = 1 << 20
OWNER_BIT = 10
OWNER = 1 << OWNER_BIT

soften = 0.02
EPS = 4.0 * soften * soften
NEG_LOG2E = -math.log2(math.e)
TWO_OVER_ROOT_PI = 2.0 / math.sqrt(math.pi)

F32, BF16, I32 = jnp.float32, jnp.bfloat16, jnp.int32

CHUNK = 8
COARSE, ROWS = 16, 48
LISTS, LEAVES_OF, SIZES, FROM, LIVE, ACTIVE, MIG, PLAN = (0, 288), (576, 848), 1120, 1128, 1144, 1145, 1161, 1177
GIVEN = PLAN - LIVE
SLOT_BIT, PLACE_BIT = 16, 5
PLACES = 1023

VMEM = pl.BlockSpec(memory_space=pltpu.VMEM)
SMEM = pl.BlockSpec(memory_space=pltpu.SMEM)
ANY = pl.BlockSpec(memory_space=pl.ANY)


def params(mib):
    return pltpu.CompilerParams(vmem_limit_bytes=mib << 20)


def swapped(shard, partner):
    return lax.ppermute(shard, "dom", [(i, partner(i) % lax.axis_size("dom")) for i in range(lax.axis_size("dom"))])


PARTNERS_OF = (
    lambda d: d + 2 if d & 2 else d - 2,
    lambda d: d + 1 if d & 1 else d - 1,
    lambda d: d ^ 2,
    lambda d: d ^ 1,
)


def swap_offsets(me):
    one, two = 1 - 2 * (me & 1), 2 - 2 * (me & 2)
    return -two, -one, two, one


def number_of(offset):
    return offset + jnp.where(offset < 0, REACH, REACH - 1)


def request_kernel(domains, leaves, me_ref, entry_ref, *outs):
    requests, place_ref = outs[:SIDES], outs[SIDES]
    entry = entry_ref[...]
    leaf = entry & (OWNER - 1)
    relative = lax.shift_right_logical(entry, OWNER_BIT) - me_ref[0] + REACH
    relative = jnp.where(relative < 0, relative + domains, relative)
    relative = jnp.where(relative >= domains, relative - domains, relative)
    lane = lax.broadcasted_iota(I32, (1, LANES), 1)
    place = IMPORTS + leaf

    def over_all(reduce, v):
        return reduce(reduce(v, axis=0, keepdims=True), axis=1, keepdims=True)

    for side, offset in enumerate(swap_offsets(me_ref[0])):
        mine = relative == offset + REACH
        low, high = jnp.where(mine, leaf, BIG), jnp.where(mine, leaf, -1)
        rank = jnp.zeros_like(leaf)
        row = jnp.zeros((1, LANES), I32)
        for k in range(IMPORT // 2):
            last = IMPORT - 1 - k
            least, most = over_all(jnp.min, low), over_all(jnp.max, high)
            row = jnp.where(lane == k, jnp.broadcast_to(least, row.shape), row)
            row = jnp.where(lane == last, jnp.broadcast_to(most, row.shape), row)
            rank = jnp.where(low == least, k, jnp.where(high == most, last, rank))
            low = jnp.where(low == least, BIG, low)
            high = jnp.where(high == most, -1, high)
        requests[side][...] = jnp.clip(row, 0, leaves - 1)
        place = jnp.where(mine, side * IMPORT + rank, place)
    place_ref[...] = place


def plan_kernel(packed_ref, given_ref, _, plan_ref):
    for i in range(GIVEN):
        plan_ref[LIVE + i] = given_ref[i]
    live = given_ref[0]

    def one_slot(a, carried):
        ends, origins = carried
        leaf = given_ref[ACTIVE - LIVE + a]
        hits = jnp.int32(0)
        found = []
        for n in range(SIDES * SLOTS):
            hit = given_ref[MIG - LIVE + n] == leaf
            found.append(jnp.where(hit, a, origins[n]))
            hits = hits + jnp.where(hit, 1, 0)
        leaves = hits > 0
        end, local_end = (jnp.where(leaves, one, other) for one, other in zip(*ends))
        leaf_base = jnp.where(leaves, *LEAVES_OF)
        for k in range(PARTNERS):
            packed = packed_ref[a, k]
            place, times = lax.shift_right_logical(packed, PLACE_BIT), packed & 31
            remote = place < IMPORTS
            row = jnp.where(remote, place, IMPORTS + local_end - leaf_base)
            plan_ref[end] = (a << SLOT_BIT) + (row << PLACE_BIT) + times
            plan_ref[local_end] = place - IMPORTS
            counts = jnp.where(times > 0, 1, 0)
            end, local_end = end + counts, local_end + jnp.where(remote, 0, counts)
        one, other = ends
        leaving = tuple(jnp.where(leaves, new, old) for new, old in zip((end, local_end), one))
        staying = tuple(jnp.where(leaves, old, new) for new, old in zip((end, local_end), other))
        return (leaving, staying), tuple(found)

    starts = tuple((jnp.int32(base), jnp.int32(leaf_base)) for base, leaf_base in zip(LISTS, LEAVES_OF))
    nowhere = tuple(jnp.int32(-1) for _ in range(SIDES * SLOTS))
    ends, origins = lax.fori_loop(0, live, one_slot, (starts, nowhere))
    for n, a in enumerate(origins):
        plan_ref[FROM + n] = a
    for i, (end, local_end) in enumerate(ends):
        for k in range(2 * CHUNK):
            plan_ref[end + k] = 0
            plan_ref[local_end + k] = 0
        plan_ref[SIZES + 2 * i] = end - LISTS[i]
        plan_ref[SIZES + 2 * i + 1] = local_end - LEAVES_OF[i]


def reply_kernel(r0, r1, r2, r3, points, o0, o1, o2, o3, token):
    token[...] = jnp.zeros_like(token)
    for request, out in ((r0, o0), (r1, o1), (r2, o2), (r3, o3)):
        for k in range(IMPORT):
            at = pl.ds(request[0, k], 1)
            for c in range(3):
                out[8 * c + k : 8 * c + k + 1, :] = 2.0 * points[c, at, :]
            out[24 + k : 25 + k, :] = points[3, at, :]


def pieces(v):
    a = v.astype(BF16).astype(F32)
    b = (v - a).astype(BF16).astype(F32)
    return a, b, v - a - b


def split_rows(xs):
    h = [jnp.floor(x * 128.0 + 0.5) * (1.0 / 128.0) for x in xs]
    l = [x - y for x, y in zip(xs, h)]
    l1 = [v.astype(BF16).astype(F32) for v in l]
    l2 = [v - w for v, w in zip(l, l1)]
    coarse = h[0] * h[0] + h[1] * h[1] + h[2] * h[2]
    fine = sum(b * (2.0 * a + b) for a, b in zip(h, l))
    return h, l1, l2, coarse, fine


def times_minus_two(rows):
    return [-2.0 * r for r in rows]


def source_rows(xs):
    h, l1, l2, coarse, fine = split_rows(xs)
    one, none = jnp.ones_like(coarse), [None]
    first = times_minus_two(h) + [*pieces(coarse), one, one, one] + none * 7
    return first + [*h, *h, *l1, *l2, *l1, *l1, *l2, *l2, *pieces(fine), one, one, one] + none * 2


def target_rows(xs):
    h, l1, l2, coarse, fine = split_rows(xs)
    one, none = jnp.ones_like(coarse), [None]
    first = h + [one, one, one, *pieces(coarse)] + none * 7
    n1, n2, nh = times_minus_two(l1), times_minus_two(l2), times_minus_two(h)
    return first + [*n1, *n2, *nh, *nh, *n1, *n2, *n1, *n2, one, one, one, *pieces(fine + EPS)] + none * 2


def by_leaf(stage, rows, start=0):
    for r, row in enumerate(rows):
        stage[pl.ds(start + r, 8, stride=len(rows)), :] = jnp.zeros((8, LANES), F32) if row is None else row


def set_sources(first, xs, m, stage, sources, blocks):
    by_leaf(stage, source_rows(xs))
    pad = jnp.zeros((LANES - ROWS, LANES), F32)
    for k in range(8):
        wide = jnp.concatenate([stage[ROWS * k : ROWS * (k + 1), :], pad], axis=0)
        sources[first + k] = jnp.transpose(wide)[:, :ROWS].astype(BF16)
    rows = [*xs, jnp.ones_like(m), m] + [None] * 3
    by_leaf(blocks, rows, start=8 * first)


def run_list(plan_ref, base, n, targets, centers, sources, blocks, sums, square, split):
    def entry(q, t):
        at = q * CHUNK + t
        word = plan_ref[base + at]
        place = lax.shift_right_logical(word, PLACE_BIT) & PLACES
        return lax.shift_right_logical(word, SLOT_BIT), place, (word & 31).astype(F32)

    def distances(q):
        for t in range(CHUNK):
            slot, place, _ = entry(q, t)
            square[t] = jnp.dot(
                sources[place, :, :COARSE], targets[slot, :COARSE], preferred_element_type=F32
            ) + jnp.dot(sources[place, :, COARSE:], targets[slot, COARSE:], preferred_element_type=F32)

    def force_law():
        for t in range(CHUNK):
            sq = square[t]
            inverse = lax.rsqrt(sq)
            gauss = TWO_OVER_ROOT_PI * jnp.exp2(sq * NEG_LOG2E)
            law = ((1.0 - lax.erf(sq * inverse)) * inverse + gauss) * (inverse * inverse)
            high = law.astype(BF16)
            split[t, :LANES] = high
            split[t, LANES:] = (law - high.astype(F32)).astype(BF16)

    def add_up(q):
        for t in range(CHUNK):
            slot, place, times = entry(q, t)
            block = blocks[pl.ds(pl.multiple_of(8 * place, 8), 8), :]
            a, b, c = pieces((block - centers[slot]) * (block[4:5] * times))
            weights = jnp.concatenate([a, b, c, jnp.zeros_like(c)], axis=0).astype(BF16)
            out = jnp.dot(jnp.concatenate([weights, weights], axis=1), split[t], preferred_element_type=F32)
            sums[slot] += out[0:8] + out[8:16] + out[16:24]

    chunks = jnp.maximum(lax.shift_right_logical(n + CHUNK - 1, 3), 2)
    distances(0)
    force_law()
    distances(1)

    @pl.loop(2, chunks)
    def _(q):
        add_up(q - 2)
        force_law()
        distances(q)

    add_up(chunks - 2)
    force_law()
    add_up(chunks - 1)


def stage_kernel(given_ref, positions_ref, masses_ref, place_ref, points, targets, centers, packed_ref, held, stage):
    place = place_ref[...]
    column = lax.broadcasted_iota(I32, place.shape, 1)
    times = jnp.zeros_like(place)
    earlier = jnp.zeros_like(place)
    for k in range(PARTNERS):
        same = (place == place[:, k : k + 1]).astype(I32)
        times = times + same
        earlier = jnp.where(column > k, earlier + same, earlier)
    packed_ref[...] = (place << PLACE_BIT) + jnp.where(earlier > 0, 0, times)
    points[:3] = positions_ref[...]
    points[3] = masses_ref[...]
    for a in range(ACT):
        at = pl.ds(given_ref[ACTIVE - LIVE + a], 1)
        for c in range(3):
            held[16 * c + a : 16 * c + a + 1, :] = 2.0 * positions_ref[c, at, :]
    for g in range(ACT // 8):
        xs = [held[16 * c + 8 * g : 16 * c + 8 * g + 8, :] for c in range(3)]
        by_leaf(stage, target_rows(xs))
        for k in range(8):
            targets[8 * g + k] = stage[ROWS * k : ROWS * (k + 1), :].astype(BF16)
        means = [jnp.broadcast_to(jnp.mean(x, axis=1, keepdims=True), x.shape) for x in xs]
        by_leaf(stage, means + [None] * 5)
        for k in range(8):
            centers[8 * g + k] = stage[8 * k : 8 * k + 8, :]


def all_pairs(which, plan_ref, points, received, targets, centers, sums, held, stage, sources, blocks, square, split):
    for side, ref in enumerate(received):
        xs = [ref[8 * c : 8 * c + 8, :] for c in range(3)]
        set_sources(8 * side, xs, ref[24:32, :], stage, sources, blocks)

    @pl.loop(0, lax.shift_right_logical(plan_ref[SIZES + 2 * which + 1] + 7, 3))
    def _(g):
        for k in range(8):
            at = pl.ds(plan_ref[LEAVES_OF[which] + 8 * g + k], 1)
            for c in range(3):
                held[8 * c + k : 8 * c + k + 1, :] = 2.0 * points[c, at, :]
            held[24 + k : 25 + k, :] = points[3, at, :]
        xs = [held[8 * c : 8 * c + 8, :] for c in range(3)]
        first = pl.multiple_of(IMPORTS + 8 * g, 8)
        set_sources(first, xs, held[24:32, :], stage, sources, blocks)

    n = plan_ref[SIZES + 2 * which]
    run_list(plan_ref, LISTS[which], n, targets, centers, sources, blocks, sums, square, split)


def kicked(x, v, total, center, c):
    return v + (total[c : c + 1] - (2.0 * x - center[c : c + 1]) * total[3:4])


def leaving_kernel(me_ref, plan_ref, points, velocities_ref, targets, centers, r0, r1, r2, r3,
                   sums, b0, b1, b2, b3, *scratch):
    sums[...] = jnp.zeros_like(sums)

    @pl.when(plan_ref[SIZES] > 0)
    def _():
        all_pairs(0, plan_ref, points, (r0, r1, r2, r3), targets, centers, sums, *scratch)

    for offset, block in zip(swap_offsets(me_ref[0]), (b0, b1, b2, b3)):
        number = SLOTS * number_of(offset)
        for k in range(SLOTS):
            leaf, a = plan_ref[MIG + number + k], plan_ref[FROM + number + k]
            at = pl.ds(jnp.maximum(leaf, 0), 1)
            held = jnp.full((1, LANES), jnp.where(leaf >= 0, 1, 0), I32) > 0
            live = jnp.full((1, LANES), jnp.where(a >= 0, 1, 0), I32) > 0
            total, center = sums[jnp.maximum(a, 0)], centers[jnp.maximum(a, 0)]
            for c in range(3):
                x, v = points[c, at, :], velocities_ref[c, at, :]
                v = jnp.where(live, kicked(x, v, total, center, c), v)
                block[c, k : k + 1, :] = jnp.where(held, x + 0.25 * v, 0.0)
                block[3 + c, k : k + 1, :] = jnp.where(held, v, 0.0)
            block[6, k : k + 1, :] = jnp.where(held, points[3, at, :], 0.0)


def staying_kernel(plan_ref, points, velocities_ref, sums_in, targets, centers, r0, r1, r2, r3,
                   new_positions, new_velocities, sums, *scratch):
    sums[...] = sums_in[...]
    new_velocities[...] = velocities_ref[...]
    new_positions[...] = points[:3] + 0.25 * velocities_ref[...]
    all_pairs(1, plan_ref, points, (r0, r1, r2, r3), targets, centers, sums, *scratch)

    @pl.loop(0, plan_ref[LIVE])
    def _(a):
        at = pl.ds(plan_ref[ACTIVE + a], 1)
        total, center = sums[a], centers[a]
        for c in range(3):
            x = points[c, at, :]
            v = kicked(x, velocities_ref[c, at, :], total, center, c)
            new_velocities[c, at, :] = v
            new_positions[c, at, :] = x + 0.25 * v


def arrival_kernel(me_ref, c0, c1, c2, c3, out):
    for offset, came in zip(swap_offsets(me_ref[0]), (c0, c1, c2, c3)):
        out[:, pl.ds(SLOTS * number_of(-offset), SLOTS), :] = came[...]


def shape(*dims, dtype=F32):
    return jax.ShapeDtypeStruct(dims, dtype)


def per_device(positions, velocities, masses, active_leaves, active_count, partner_owner, partner_leaf, mig_leaf):
    leaves = positions.shape[1]
    domains = lax.axis_size("dom")
    me = lax.axis_index("dom").astype(I32)
    *requests, place = pl.pallas_call(
        functools.partial(request_kernel, domains, leaves),
        out_shape=[shape(1, LANES, dtype=I32)] * SIDES + [shape(ACT, PARTNERS, dtype=I32)],
        in_specs=[SMEM, VMEM],
        out_specs=[VMEM] * (SIDES + 1),
        compiler_params=params(4),
        cost_estimate=pl.CostEstimate(flops=3_000_000_000, bytes_accessed=10_000, transcendentals=0),
        name="requests",
    )(me.reshape(1), partner_owner * OWNER + partner_leaf)
    asked = [swapped(r, p) for r, p in zip(requests, PARTNERS_OF)]
    stage = [pltpu.VMEM((8 * ROWS, LANES), F32)]
    chunks = [pltpu.VMEM((CHUNK, LANES, LANES), F32), pltpu.VMEM((CHUNK, 2 * LANES, LANES), BF16)]
    slot_sums, most = shape(ACT, 8, LANES), IMPORTS + ACT * PARTNERS
    held = [pltpu.VMEM((48, LANES), F32)]
    given = jnp.concatenate([active_count, active_leaves, mig_leaf])
    points, targets, centers, packed = pl.pallas_call(
        stage_kernel,
        out_shape=[
            shape(4, leaves, LANES),
            shape(ACT, ROWS, LANES, dtype=BF16),
            slot_sums,
            shape(ACT, PARTNERS, dtype=I32),
        ],
        in_specs=[SMEM] + [VMEM] * 3,
        out_specs=[VMEM] * 4,
        scratch_shapes=held + stage,
        compiler_params=params(8),
        cost_estimate=pl.CostEstimate(flops=3_000_000_000, bytes_accessed=10_000, transcendentals=0),
        name="stage",
    )(given, positions, masses, place)
    *replies, token = pl.pallas_call(
        reply_kernel,
        out_shape=[shape(4 * IMPORT, LANES)] * SIDES + [shape(1, LANES)],
        in_specs=[SMEM] * SIDES + [VMEM],
        out_specs=[VMEM] * (SIDES + 1),
        compiler_params=params(4),
        name="replies",
    )(*asked, points)
    received = [swapped(r, p) for r, p in zip(replies, PARTNERS_OF)]
    plan = pl.pallas_call(
        plan_kernel,
        out_shape=shape(PLAN, dtype=I32),
        in_specs=[SMEM] * 2 + [ANY],
        out_specs=SMEM,
        compiler_params=params(4),
        cost_estimate=pl.CostEstimate(flops=2_000_000_000, bytes_accessed=10_000, transcendentals=0),
        name="plan",
    )(packed, given, token)
    tables = [pltpu.VMEM((most, LANES, ROWS), BF16), pltpu.VMEM((8 * most, LANES), F32)]
    sums, *blocks = pl.pallas_call(
        leaving_kernel,
        out_shape=[slot_sums] + [shape(7, SLOTS, LANES)] * SIDES,
        in_specs=[SMEM] * 2 + [VMEM] * (4 + SIDES),
        out_specs=[VMEM] * (1 + SIDES),
        scratch_shapes=held + stage + tables + chunks,
        compiler_params=params(24),
        name="leaving",
    )(me.reshape(1), plan, points, velocities, targets, centers, *received)
    came = [swapped(b, p) for b, p in zip(blocks, PARTNERS_OF)]
    new_positions, new_velocities = pl.pallas_call(
        staying_kernel,
        out_shape=[shape(3, leaves, LANES)] * 2,
        in_specs=[SMEM] + [VMEM] * (5 + SIDES),
        out_specs=[VMEM] * 2,
        scratch_shapes=[pltpu.VMEM((ACT, 8, LANES), F32)] + held + stage + tables + chunks,
        compiler_params=params(24),
        cost_estimate=pl.CostEstimate(flops=7_000_000_000, bytes_accessed=10_000, transcendentals=0),
        name="staying",
    )(plan, points, velocities, sums, targets, centers, *received)
    arrived = pl.pallas_call(
        arrival_kernel,
        out_shape=shape(7, SIDES * SLOTS, LANES),
        in_specs=[SMEM] + [VMEM] * SIDES,
        out_specs=VMEM,
        compiler_params=params(4),
        name="arrivals",
    )(me.reshape(1), *came)
    return new_positions, new_velocities, arrived


def solution(mesh):
    return jax.shard_map(
        per_device,
        mesh=mesh,
        in_specs=(
            P(None, "dom", None),
            P(None, "dom", None),
            P("dom", None),
            P("dom"),
            P("dom"),
            P("dom", None),
            P("dom", None),
            P("dom"),
        ),
        out_specs=(P(None, "dom", None), P(None, "dom", None), P(None, "dom", None)),
        check_vma=False,
    )
```

```python
import functools
import math

import jax
import jax.numpy as jnp
from jax import lax
from jax.experimental import pallas as pl
from jax.experimental.pallas import tpu as pltpu
from jax.sharding import PartitionSpec as P

REACH = 2
SLOTS = 4
IMPORT = 8
ACT = 16
PARTNERS = 16
LANES = 128
SIDES = 2 * REACH
IMPORTS = SIDES * IMPORT
BIG = 1 << 20
OWNER_BIT = 10
OWNER = 1 << OWNER_BIT

soften = 0.02
EPS = 4.0 * soften * soften
NEG_LOG2E = -math.log2(math.e)
TWO_OVER_ROOT_PI = 2.0 / math.sqrt(math.pi)

F32, BF16, I32 = jnp.float32, jnp.bfloat16, jnp.int32

CHUNK = 8
COARSE, ROWS = 16, 48
LISTS, LEAVES_OF, SIZES, FROM, LIVE, ACTIVE, MIG, PLAN = (0, 288, 576), (864, 1136, 1408), 1680, 1688, 1704, 1705, 1721, 1737
LEAVING, STAYING, EARLY = range(3)
GIVEN = PLAN - LIVE
SLOT_BIT, PLACE_BIT = 16, 5
PLACES = 1023

VMEM = pl.BlockSpec(memory_space=pltpu.VMEM)
SMEM = pl.BlockSpec(memory_space=pltpu.SMEM)
ANY = pl.BlockSpec(memory_space=pl.ANY)


def params(mib):
    return pltpu.CompilerParams(vmem_limit_bytes=mib << 20)


def swapped(shard, partner):
    return lax.ppermute(shard, "dom", [(i, partner(i) % lax.axis_size("dom")) for i in range(lax.axis_size("dom"))])


PARTNERS_OF = (
    lambda d: d + 2 if d & 2 else d - 2,
    lambda d: d + 1 if d & 1 else d - 1,
    lambda d: d ^ 2,
    lambda d: d ^ 1,
)


def swap_offsets(me):
    one, two = 1 - 2 * (me & 1), 2 - 2 * (me & 2)
    return -two, -one, two, one


def number_of(offset):
    return offset + jnp.where(offset < 0, REACH, REACH - 1)


def request_kernel(domains, leaves, me_ref, entry_ref, *outs):
    requests, place_ref = outs[:SIDES], outs[SIDES]
    entry = entry_ref[...]
    leaf = entry & (OWNER - 1)
    relative = lax.shift_right_logical(entry, OWNER_BIT) - me_ref[0] + REACH
    relative = jnp.where(relative < 0, relative + domains, relative)
    relative = jnp.where(relative >= domains, relative - domains, relative)
    lane = lax.broadcasted_iota(I32, (1, LANES), 1)
    place = IMPORTS + leaf

    def over_all(reduce, v):
        return reduce(reduce(v, axis=0, keepdims=True), axis=1, keepdims=True)

    for side, offset in enumerate(swap_offsets(me_ref[0])):
        mine = relative == offset + REACH
        low, high = jnp.where(mine, leaf, BIG), jnp.where(mine, leaf, -1)
        rank = jnp.zeros_like(leaf)
        row = jnp.zeros((1, LANES), I32)
        for k in range(IMPORT // 2):
            last = IMPORT - 1 - k
            least, most = over_all(jnp.min, low), over_all(jnp.max, high)
            row = jnp.where(lane == k, jnp.broadcast_to(least, row.shape), row)
            row = jnp.where(lane == last, jnp.broadcast_to(most, row.shape), row)
            rank = jnp.where(low == least, k, jnp.where(high == most, last, rank))
            low = jnp.where(low == least, BIG, low)
            high = jnp.where(high == most, -1, high)
        requests[side][...] = jnp.clip(row, 0, leaves - 1)
        place = jnp.where(mine, side * IMPORT + rank, place)
    place_ref[...] = place


def early_place(me):
    place = me & 7
    return (place == 0) | ((place > 1) & (place < 6))


def make_plan(early, packed_ref, given_ref, plan_ref):
    live = given_ref[0]

    def one_slot(a, carried):
        ends, origins = carried
        leaf = given_ref[ACTIVE - LIVE + a]
        hits = jnp.int32(0)
        found = []
        for n in range(SIDES * SLOTS):
            hit = given_ref[MIG - LIVE + n] == leaf
            found.append(jnp.where(hit, a, origins[n]))
            hits = hits + jnp.where(hit, 1, 0)
        leaves = hits > 0
        slot = a << SLOT_BIT
        one, other, local = ends
        end, local_end = (jnp.where(leaves, *two) for two in zip(one, other))
        leaf_base = jnp.where(leaves, *LEAVES_OF[:2])
        own_end = local[0]
        if early:
            local_end, leaf_base = local[1], LEAVES_OF[EARLY]
        for k in range(PARTNERS):
            packed = packed_ref[a, k]
            counts = jnp.where((packed & 31) > 0, 1, 0)
            remote = packed < (IMPORTS << PLACE_BIT)
            own = jnp.where(remote, 0, counts)
            at_home = slot + ((IMPORTS + local_end - leaf_base) << PLACE_BIT) + (packed & 31)
            plan_ref[local_end] = lax.shift_right_logical(packed, PLACE_BIT) - IMPORTS
            if early:
                plan_ref[end] = slot + packed
                plan_ref[own_end] = at_home
                end, own_end = end + counts - own, own_end + own
            else:
                plan_ref[end] = jnp.where(remote, slot + packed, at_home)
                end = end + counts
            local_end = local_end + own
        if early:
            local, now = (own_end, local_end), (end, one[1])
        else:
            now = (end, local_end)
        one = tuple(jnp.where(leaves, new, old) for new, old in zip(now, one))
        other = tuple(jnp.where(leaves, old, new) for new, old in zip(now, other))
        return (one, other, local), tuple(found)

    starts = tuple((jnp.int32(base), jnp.int32(leaf_base)) for base, leaf_base in zip(LISTS, LEAVES_OF))
    nowhere = tuple(jnp.int32(-1) for _ in range(SIDES * SLOTS))
    ends, origins = lax.fori_loop(0, live, one_slot, (starts, nowhere))
    for n, a in enumerate(origins):
        plan_ref[FROM + n] = a
    for i, (end, local_end) in enumerate(ends):
        if early and i != EARLY:
            local_end = jnp.int32(LEAVES_OF[i])
        for k in range(2 * CHUNK):
            plan_ref[end + k] = IMPORTS << PLACE_BIT if i == EARLY else 0
            plan_ref[local_end + k] = 0
        plan_ref[SIZES + 2 * i] = end - LISTS[i]
        plan_ref[SIZES + 2 * i + 1] = local_end - LEAVES_OF[i]


def plan_kernel(me_ref, packed_ref, given_ref, points, targets, centers, _, plan_ref, sums, *scratch):
    for i in range(GIVEN):
        plan_ref[LIVE + i] = given_ref[i]
    sums[...] = jnp.zeros_like(sums)
    early = early_place(me_ref[0])

    @pl.when(early)
    def _():
        make_plan(True, packed_ref, given_ref, plan_ref)

        @pl.when(plan_ref[SIZES + 2 * EARLY] > 0)
        def _():
            all_pairs(EARLY, plan_ref, points, (), targets, centers, sums, *scratch)

    @pl.when(jnp.logical_not(early))
    def _():
        make_plan(False, packed_ref, given_ref, plan_ref)


def reply_kernel(r0, r1, r2, r3, points, o0, o1, o2, o3, token):
    token[...] = jnp.zeros_like(token)
    for request, out in ((r0, o0), (r1, o1), (r2, o2), (r3, o3)):
        for k in range(IMPORT):
            at = pl.ds(request[0, k], 1)
            for c in range(3):
                out[8 * c + k : 8 * c + k + 1, :] = 2.0 * points[c, at, :]
            out[24 + k : 25 + k, :] = points[3, at, :]


def pieces(v):
    a = v.astype(BF16).astype(F32)
    b = (v - a).astype(BF16).astype(F32)
    return a, b, v - a - b


def split_rows(xs):
    h = [jnp.floor(x * 128.0 + 0.5) * (1.0 / 128.0) for x in xs]
    l = [x - y for x, y in zip(xs, h)]
    l1 = [v.astype(BF16).astype(F32) for v in l]
    l2 = [v - w for v, w in zip(l, l1)]
    coarse = h[0] * h[0] + h[1] * h[1] + h[2] * h[2]
    fine = sum(b * (2.0 * a + b) for a, b in zip(h, l))
    return h, l1, l2, coarse, fine


def times_minus_two(rows):
    return [-2.0 * r for r in rows]


def source_rows(xs):
    h, l1, l2, coarse, fine = split_rows(xs)
    one, none = jnp.ones_like(coarse), [None]
    first = times_minus_two(h) + [*pieces(coarse), one, one, one] + none * 7
    return first + [*h, *h, *l1, *l2, *l1, *l1, *l2, *l2, *pieces(fine), one, one, one] + none * 2


def target_rows(xs):
    h, l1, l2, coarse, fine = split_rows(xs)
    one, none = jnp.ones_like(coarse), [None]
    first = h + [one, one, one, *pieces(coarse)] + none * 7
    n1, n2, nh = times_minus_two(l1), times_minus_two(l2), times_minus_two(h)
    return first + [*n1, *n2, *nh, *nh, *n1, *n2, *n1, *n2, one, one, one, *pieces(fine + EPS)] + none * 2


def by_leaf(stage, rows, start=0):
    for r, row in enumerate(rows):
        stage[pl.ds(start + r, 8, stride=len(rows)), :] = jnp.zeros((8, LANES), F32) if row is None else row


def set_sources(first, xs, m, stage, sources, blocks):
    by_leaf(stage, source_rows(xs))
    for k in range(8):
        sources[first + k] = jnp.transpose(stage[ROWS * k : ROWS * (k + 1), :]).astype(BF16)
    rows = [*xs, jnp.ones_like(m), m] + [None] * 3
    by_leaf(blocks, rows, start=8 * first)


def run_list(plan_ref, base, n, targets, centers, sources, blocks, sums, square, split):
    def entry(q, t):
        at = q * CHUNK + t
        word = plan_ref[base + at]
        place = lax.shift_right_logical(word, PLACE_BIT) & PLACES
        return lax.shift_right_logical(word, SLOT_BIT), place, (word & 31).astype(F32)

    def distances(q):
        for t in range(CHUNK):
            slot, place, _ = entry(q, t)
            square[t] = jnp.dot(
                sources[place, :, :COARSE], targets[slot, :COARSE], preferred_element_type=F32
            ) + jnp.dot(sources[place, :, COARSE:], targets[slot, COARSE:], preferred_element_type=F32)

    def force_law():
        for t in range(CHUNK):
            sq = square[t]
            inverse = lax.rsqrt(sq)
            gauss = TWO_OVER_ROOT_PI * jnp.exp2(sq * NEG_LOG2E)
            law = ((1.0 - lax.erf(sq * inverse)) * inverse + gauss) * (inverse * inverse)
            high = law.astype(BF16)
            split[t, :LANES] = high
            split[t, LANES:] = (law - high.astype(F32)).astype(BF16)

    def add_up(q):
        for t in range(CHUNK):
            slot, place, times = entry(q, t)
            block = blocks[pl.ds(pl.multiple_of(8 * place, 8), 8), :]
            a, b, c = pieces((block - centers[slot]) * (block[4:5] * times))
            weights = jnp.concatenate([a, b, c, jnp.zeros_like(c)], axis=0).astype(BF16)
            out = jnp.dot(jnp.concatenate([weights, weights], axis=1), split[t], preferred_element_type=F32)
            sums[slot] += out[0:8] + out[8:16] + out[16:24]

    chunks = jnp.maximum(lax.shift_right_logical(n + CHUNK - 1, 3), 2)
    distances(0)
    force_law()
    distances(1)

    @pl.loop(2, chunks)
    def _(q):
        add_up(q - 2)
        force_law()
        distances(q)

    add_up(chunks - 2)
    force_law()
    add_up(chunks - 1)


def stage_kernel(given_ref, positions_ref, masses_ref, place_ref, points, targets, centers, packed_ref, held, stage):
    place = place_ref[...]
    column = lax.broadcasted_iota(I32, place.shape, 1)
    times = jnp.zeros_like(place)
    earlier = jnp.zeros_like(place)
    for k in range(PARTNERS):
        same = (place == place[:, k : k + 1]).astype(I32)
        times = times + same
        earlier = jnp.where(column > k, earlier + same, earlier)
    packed_ref[...] = (place << PLACE_BIT) + jnp.where(earlier > 0, 0, times)
    points[:3] = positions_ref[...]
    points[3] = masses_ref[...]
    for a in range(ACT):
        at = pl.ds(given_ref[ACTIVE - LIVE + a], 1)
        for c in range(3):
            held[16 * c + a : 16 * c + a + 1, :] = 2.0 * positions_ref[c, at, :]
    for g in range(ACT // 8):
        xs = [held[16 * c + 8 * g : 16 * c + 8 * g + 8, :] for c in range(3)]
        by_leaf(stage, target_rows(xs))
        for k in range(8):
            targets[8 * g + k] = stage[ROWS * k : ROWS * (k + 1), :].astype(BF16)
        means = [jnp.broadcast_to(jnp.mean(x, axis=1, keepdims=True), x.shape) for x in xs]
        by_leaf(stage, means + [None] * 5)
        for k in range(8):
            centers[8 * g + k] = stage[8 * k : 8 * k + 8, :]


def all_pairs(which, plan_ref, points, received, targets, centers, sums, held, stage, sources, blocks, square, split):
    for side, ref in enumerate(received):
        xs = [ref[8 * c : 8 * c + 8, :] for c in range(3)]
        set_sources(8 * side, xs, ref[24:32, :], stage, sources, blocks)

    @pl.loop(0, lax.shift_right_logical(plan_ref[SIZES + 2 * which + 1] + 7, 3))
    def _(g):
        for k in range(8):
            at = pl.ds(plan_ref[LEAVES_OF[which] + 8 * g + k], 1)
            for c in range(3):
                held[8 * c + k : 8 * c + k + 1, :] = 2.0 * points[c, at, :]
            held[24 + k : 25 + k, :] = points[3, at, :]
        xs = [held[8 * c : 8 * c + 8, :] for c in range(3)]
        first = pl.multiple_of(IMPORTS + 8 * g, 8)
        set_sources(first, xs, held[24:32, :], stage, sources, blocks)

    n = plan_ref[SIZES + 2 * which]
    run_list(plan_ref, LISTS[which], n, targets, centers, sources, blocks, sums, square, split)


def kicked(x, v, total, center, c):
    return v + (total[c : c + 1] - (2.0 * x - center[c : c + 1]) * total[3:4])


def leaving_kernel(me_ref, plan_ref, points, velocities_ref, sums_in, targets, centers, r0, r1, r2, r3,
                   sums, b0, b1, b2, b3, *scratch):
    sums[...] = sums_in[...]

    @pl.when(plan_ref[SIZES] > 0)
    def _():
        all_pairs(LEAVING, plan_ref, points, (r0, r1, r2, r3), targets, centers, sums, *scratch)

    for offset, block in zip(swap_offsets(me_ref[0]), (b0, b1, b2, b3)):
        number = SLOTS * number_of(offset)
        for k in range(SLOTS):
            leaf, a = plan_ref[MIG + number + k], plan_ref[FROM + number + k]
            at = pl.ds(jnp.maximum(leaf, 0), 1)
            held = jnp.full((1, LANES), jnp.where(leaf >= 0, 1, 0), I32) > 0
            live = jnp.full((1, LANES), jnp.where(a >= 0, 1, 0), I32) > 0
            total, center = sums[jnp.maximum(a, 0)], centers[jnp.maximum(a, 0)]
            for c in range(3):
                x, v = points[c, at, :], velocities_ref[c, at, :]
                v = jnp.where(live, kicked(x, v, total, center, c), v)
                block[c, k : k + 1, :] = jnp.where(held, x + 0.25 * v, 0.0)
                block[3 + c, k : k + 1, :] = jnp.where(held, v, 0.0)
            block[6, k : k + 1, :] = jnp.where(held, points[3, at, :], 0.0)


def staying_kernel(plan_ref, points, velocities_ref, sums_in, targets, centers, r0, r1, r2, r3,
                   new_positions, new_velocities, sums, *scratch):
    sums[...] = sums_in[...]
    new_velocities[...] = velocities_ref[...]
    new_positions[...] = points[:3] + 0.25 * velocities_ref[...]
    all_pairs(STAYING, plan_ref, points, (r0, r1, r2, r3), targets, centers, sums, *scratch)

    @pl.loop(0, plan_ref[LIVE])
    def _(a):
        at = pl.ds(plan_ref[ACTIVE + a], 1)
        total, center = sums[a], centers[a]
        for c in range(3):
            x = points[c, at, :]
            v = kicked(x, velocities_ref[c, at, :], total, center, c)
            new_velocities[c, at, :] = v
            new_positions[c, at, :] = x + 0.25 * v


def arrival_kernel(me_ref, c0, c1, c2, c3, out):
    for offset, came in zip(swap_offsets(me_ref[0]), (c0, c1, c2, c3)):
        out[:, pl.ds(SLOTS * number_of(-offset), SLOTS), :] = came[...]


def shape(*dims, dtype=F32):
    return jax.ShapeDtypeStruct(dims, dtype)


def per_device(positions, velocities, masses, active_leaves, active_count, partner_owner, partner_leaf, mig_leaf):
    leaves = positions.shape[1]
    domains = lax.axis_size("dom")
    me = lax.axis_index("dom").astype(I32)
    *requests, place = pl.pallas_call(
        functools.partial(request_kernel, domains, leaves),
        out_shape=[shape(1, LANES, dtype=I32)] * SIDES + [shape(ACT, PARTNERS, dtype=I32)],
        in_specs=[SMEM, VMEM],
        out_specs=[VMEM] * (SIDES + 1),
        compiler_params=params(4),
        cost_estimate=pl.CostEstimate(flops=3_000_000_000, bytes_accessed=10_000, transcendentals=0),
        name="requests",
    )(me.reshape(1), partner_owner * OWNER + partner_leaf)
    asked = [swapped(r, p) for r, p in zip(requests, PARTNERS_OF)]
    stage = [pltpu.VMEM((8 * ROWS, LANES), F32)]
    chunks = [pltpu.VMEM((CHUNK, LANES, LANES), F32), pltpu.VMEM((CHUNK, 2 * LANES, LANES), BF16)]
    slot_sums, most = shape(ACT, 8, LANES), IMPORTS + ACT * PARTNERS
    held = [pltpu.VMEM((48, LANES), F32)]
    given = jnp.concatenate([active_count, active_leaves, mig_leaf])
    points, targets, centers, packed = pl.pallas_call(
        stage_kernel,
        out_shape=[
            shape(4, leaves, LANES),
            shape(ACT, ROWS, LANES, dtype=BF16),
            slot_sums,
            shape(ACT, PARTNERS, dtype=I32),
        ],
        in_specs=[SMEM] + [VMEM] * 3,
        out_specs=[VMEM] * 4,
        scratch_shapes=held + stage,
        compiler_params=params(8),
        cost_estimate=pl.CostEstimate(flops=3_000_000_000, bytes_accessed=10_000, transcendentals=0),
        name="stage",
    )(given, positions, masses, place)
    *replies, token = pl.pallas_call(
        reply_kernel,
        out_shape=[shape(4 * IMPORT, LANES)] * SIDES + [shape(1, LANES)],
        in_specs=[SMEM] * SIDES + [VMEM],
        out_specs=[VMEM] * (SIDES + 1),
        compiler_params=params(4),
        name="replies",
    )(*asked, points)
    received = [swapped(r, p) for r, p in zip(replies, PARTNERS_OF)]
    tables = [pltpu.VMEM((most, LANES, ROWS), BF16), pltpu.VMEM((8 * most, LANES), F32)]
    plan, sums = pl.pallas_call(
        plan_kernel,
        out_shape=[shape(PLAN, dtype=I32), slot_sums],
        in_specs=[SMEM] * 3 + [VMEM] * 3 + [ANY],
        out_specs=[SMEM, VMEM],
        scratch_shapes=held + stage + tables + chunks,
        compiler_params=params(24),
        cost_estimate=pl.CostEstimate(flops=4_000_000_000, bytes_accessed=10_000, transcendentals=0),
        name="plan",
    )(me.reshape(1), packed, given, points, targets, centers, token)
    sums, *blocks = pl.pallas_call(
        leaving_kernel,
        out_shape=[slot_sums] + [shape(7, SLOTS, LANES)] * SIDES,
        in_specs=[SMEM] * 2 + [VMEM] * (5 + SIDES),
        out_specs=[VMEM] * (1 + SIDES),
        scratch_shapes=held + stage + tables + chunks,
        compiler_params=params(24),
        name="leaving",
    )(me.reshape(1), plan, points, velocities, sums, targets, centers, *received)
    came = [swapped(b, p) for b, p in zip(blocks, PARTNERS_OF)]
    new_positions, new_velocities = pl.pallas_call(
        staying_kernel,
        out_shape=[shape(3, leaves, LANES)] * 2,
        in_specs=[SMEM] + [VMEM] * (5 + SIDES),
        out_specs=[VMEM] * 2,
        scratch_shapes=[pltpu.VMEM((ACT, 8, LANES), F32)] + held + stage + tables + chunks,
        compiler_params=params(24),
        cost_estimate=pl.CostEstimate(flops=7_000_000_000, bytes_accessed=10_000, transcendentals=0),
        name="staying",
    )(plan, points, velocities, sums, targets, centers, *received)
    arrived = pl.pallas_call(
        arrival_kernel,
        out_shape=shape(7, SIDES * SLOTS, LANES),
        in_specs=[SMEM] + [VMEM] * SIDES,
        out_specs=VMEM,
        compiler_params=params(4),
        name="arrivals",
    )(me.reshape(1), *came)
    return new_positions, new_velocities, arrived


def solution(mesh):
    return jax.shard_map(
        per_device,
        mesh=mesh,
        in_specs=(
            P(None, "dom", None),
            P(None, "dom", None),
            P("dom", None),
            P("dom"),
            P("dom"),
            P("dom", None),
            P("dom", None),
            P("dom"),
        ),
        out_specs=(P(None, "dom", None), P(None, "dom", None), P(None, "dom", None)),
        check_vma=False,
    )
```
